256 devices in a mesh: lat: 64 (over z, y, core), lon: 4 (over x).
Axes of the slice: x: 4, y: 4, z: 8, core: 2. Of those that a mesh axis runs over, the one named last changes fastest.
Arguments:
- field: bfloat16 [512, 1440, 256], P('lat', 'lon'), may hold values from -6 to 6
- cotangent: bfloat16 [512, 1440, 256], P('lat', 'lon'), may hold values from -0.118585412 to 0.118585412
- legendre: bfloat16 [384, 512, 384], P('lat'), may hold values from -0.25 to 0.25
- quad_weight: float32 [512], P('lat'), may hold values from 0.25 to 2
- order_slots: int32 [384], replicated, may hold values from 0 to 383, as said below
- support_blocks: int32 [64, 3], P('lat'), may hold values from 0 to 63, as said below
- filter_values: bfloat16 [3, 512, 3, 8], P(None, 'lat'), may hold values from -1.25 to 1.25
- spectral_weight: bfloat16 [2, 256, 256], replicated, may hold values from -0.25 to 0.25
- disco_weight: bfloat16 [3, 256, 256], replicated, may hold values from -0.21875 to 0.21875
Outputs:
- output: bfloat16 [512, 1440, 256], P('lat', 'lon')
- grad_spectral: float32 [2, 256, 256], replicated
- grad_disco: float32 [3, 256, 256], replicated
The draws below stay inside these ranges and needn't reach their ends.
Inputs may be any that keep to these rules, and one draw needn't show every extreme that they name: order_slots holds every order from 0 to 383 exactly once; the first slot of each block of 384 // 64 slots holds an order below 64. `support_blocks`: slot 0 of row block b names b itself; slots 1 and 2 name b - 1, b or b + 1.
All inputs are finite; a program needn't handle non-finite values.
Results may differ from the reference program's by a relative error of at most 0.015.
Values may be sent and summed in bfloat16 or wider, within the bound.
No kernel may reach another device: no remote copies, remote signals or barrier semaphores. Data moves between devices by JAX's collectives and lax.ppermute only.
A program may use at most 128 MiB of HBM per device.

```python
import math
import jax
import jax.numpy as jnp
from jax import lax

C = 256
NLON = 1440
MMAX = 384
LMAX = 384
LAT_DEV = 8
NLAT = 512
LBLOCKS = 64


def draw_order_slots(key, part):
    key = jax.random.fold_in(key, 23)
    low_key = jax.random.fold_in(key, 1)
    rest_key = jax.random.fold_in(key, 2)
    per_block = MMAX // LBLOCKS
    low_orders = jax.random.permutation(low_key, jnp.arange(LBLOCKS, dtype=jnp.int32))
    rest_orders = jax.random.permutation(rest_key, jnp.arange(LBLOCKS, MMAX, dtype=jnp.int32))
    rest_orders = rest_orders.reshape(LBLOCKS, per_block - 1)
    table = jnp.concatenate([low_orders[:, None], rest_orders], axis=1)
    return table.reshape(MMAX).astype(jnp.int32)


def draw_support_blocks(key, part):
    key = jax.random.fold_in(key, 11)
    rows = jnp.arange(LBLOCKS, dtype=jnp.int32)
    offsets = jax.random.randint(key, (LBLOCKS, 2), -1, 2, dtype=jnp.int32)
    others = jnp.clip(rows[:, None] + offsets, 0, LBLOCKS - 1)
    return jnp.concatenate([rows[:, None], others], axis=1).astype(jnp.int32)


def draw_cotangent(key, part):
    key = jax.random.fold_in(key, 37)
    values = jnp.clip(jax.random.normal(key, (NLAT, NLON, C), jnp.float32), -6.0, 6.0)
    band = (jnp.arange(NLAT, dtype=jnp.int32) // LAT_DEV).astype(jnp.float32)
    rows = jnp.exp(band / (LBLOCKS - 1.0) * jnp.log(3.0))
    scale = 1.0 / jnp.sqrt(2.0 * LAT_DEV * NLON)
    return (values * rows[:, None, None] * scale).astype(jnp.bfloat16)


def level_of(stream_key, extent, cuts, low, largest):
    loudness, own = 1.0, jax.random.fold_in(stream_key, 6)
    for dim, parts in cuts:
        heights = jnp.exp(jax.random.uniform(jax.random.fold_in(own, dim), (parts,), jnp.float32, low / len(cuts), largest / len(cuts)))
        loudness = loudness * jnp.repeat(heights, extent[dim] // parts).reshape([-1 if axis == dim else 1 for axis in range(len(extent))])
    return loudness


def noise(rng, extent, width, reach, pieces=(), kind=jnp.bfloat16):
    values = width * jax.random.normal(rng, extent, jnp.float32)
    if pieces:
        values = values * level_of(rng, extent, pieces, -0.22, 0.18)
    return jnp.clip(values, -reach, reach).astype(kind)


def setup_inputs(seed: int = 0) -> dict:
    splits = jax.random.split(jax.random.key(seed), 10)
    return {
        "field": noise(splits[0], (NLAT, NLON, C), 1.0, 6.0, ((0, 64), (1, 4))),
        "cotangent": draw_cotangent(jax.random.fold_in(splits[9], 71), 0),
        "legendre": noise(splits[2], (MMAX, NLAT, LMAX), NLAT ** -0.5, 0.25, ((0, 64),)),
        "quad_weight": jnp.clip(jnp.exp(math.log(2.0) - 2.0794415 * jax.random.uniform(splits[3], (NLAT,), jnp.float32) ** level_of(splits[3], (NLAT,), ((0, 64),), -0.2, 0.2)), 0.25, 2.0),
        "order_slots": draw_order_slots(jax.random.fold_in(splits[9], 71), 0),
        "support_blocks": draw_support_blocks(jax.random.fold_in(splits[9], 71), 0),
        "filter_values": noise(splits[6], (3, NLAT, 3, LAT_DEV), (3 * LAT_DEV) ** -0.5, 1.25, ((1, 64),)),
        "spectral_weight": noise(splits[7], (2, C, C), (2 * C) ** -0.5, 0.25),
        "disco_weight": noise(splits[8], (3, C, C), (3 * C) ** -0.5, 0.21875),
    }


def fourier_tables(order_slots, nlon):
    column = jnp.arange(nlon, dtype=jnp.int32)
    phase = column[:, None] * order_slots.astype(jnp.int32)[None, :] % nlon
    angle = phase.astype(jnp.float32) * (2.0 * jnp.pi / nlon)
    cosine = jnp.cos(angle)
    sine = jnp.sin(angle)
    factor = jnp.where(order_slots == 0, 1.0, 2.0).astype(jnp.float32)[None, :]
    analysis_table = jnp.concatenate([cosine / nlon, -sine / nlon], axis=1).astype(jnp.bfloat16)
    synthesis_table = jnp.concatenate([factor * cosine, -factor * sine], axis=1).astype(jnp.bfloat16)
    return (analysis_table, synthesis_table)

def reference(field, cotangent, legendre, quad_weight, order_slots, support_blocks, filter_values, spectral_weight, disco_weight):
    f32 = jnp.float32
    bf16 = jnp.bfloat16
    analysis_table, synthesis_table = fourier_tables(order_slots, NLON)
    degree_mask = (jnp.arange(LMAX, dtype=jnp.int32)[None, :] >= order_slots[:, None]).astype(f32)
    legendre_full = legendre.astype(f32)

    def longitude(values, table):
        flat = values.transpose(0, 2, 1).reshape(NLAT * C, NLON)
        return jnp.dot(flat, table, preferred_element_type=f32).reshape(NLAT, C, 2, MMAX)

    def project(spec):
        coeffs = jnp.einsum('kal,acrk->klrc', legendre_full, spec.astype(f32))
        return (coeffs * degree_mask[:, :, None, None]).astype(bf16)
    spectrum = (longitude(field, analysis_table) * quad_weight[:, None, None, None]).astype(bf16)
    coeffs = project(spectrum)
    real_part = coeffs[:, :, 0].reshape(-1, C)
    imag_part = coeffs[:, :, 1].reshape(-1, C)
    w_real = spectral_weight[0]
    w_imag = spectral_weight[1]
    out_real = jnp.dot(real_part, w_real, preferred_element_type=f32) - jnp.dot(imag_part, w_imag, preferred_element_type=f32)
    out_imag = jnp.dot(real_part, w_imag, preferred_element_type=f32) + jnp.dot(imag_part, w_real, preferred_element_type=f32)
    mixed = jnp.stack([out_real.reshape(MMAX, LMAX, C), out_imag.reshape(MMAX, LMAX, C)], axis=2).astype(bf16)
    masked = mixed.astype(f32) * degree_mask[:, :, None, None]
    grid_spectrum = jnp.einsum('kal,klrc->arkc', legendre_full, masked).astype(bf16)
    flat_grid = grid_spectrum.reshape(NLAT, 2 * MMAX, C).transpose(0, 2, 1).reshape(NLAT * C, 2 * MMAX)
    spectral_out = jnp.dot(flat_grid, synthesis_table.T, preferred_element_type=f32)
    spectral_out = spectral_out.reshape(NLAT, C, NLON).transpose(0, 2, 1).astype(bf16)
    padded = jnp.concatenate([field[:, -1:], field, field[:, :1]], axis=1)
    padded = jnp.pad(padded, ((LAT_DEV, LAT_DEV), (0, 0), (0, 0)))
    block_ids = jnp.arange(LBLOCKS, dtype=jnp.int32)
    picks = support_blocks - block_ids[:, None] + 1
    onehot = (picks[:, :, None] == jnp.arange(3, dtype=jnp.int32)[None, None, :]).astype(f32)
    psi = filter_values.astype(f32).reshape(3, LBLOCKS, LAT_DEV, 3, LAT_DEV)
    operators = jnp.einsum('tnasb,nsq->ntaqb', psi, onehot).reshape(LBLOCKS, 3, LAT_DEV, 3 * LAT_DEV).astype(bf16)

    def responses(block):
        window_rows = lax.dynamic_slice_in_dim(padded, (block * LAT_DEV).astype(jnp.int32), 3 * LAT_DEV, 0)
        block_ops = operators[block]
        result = []
        for tap in range(3):
            piece = jnp.einsum('ab,boc->aoc', block_ops[tap].astype(f32), window_rows[:, tap:tap + NLON].astype(f32))
            result.append(piece.astype(bf16))
        return result

    def disco_block(block):
        resp = responses(block)
        total = jnp.zeros((LAT_DEV * NLON, C), f32)
        for tap in range(3):
            total = total + jnp.dot(resp[tap].reshape(-1, C), disco_weight[tap], preferred_element_type=f32)
        return total.reshape(LAT_DEV, NLON, C)
    disco_sum = lax.map(disco_block, block_ids).reshape(NLAT, NLON, C)
    pre_act = spectral_out.astype(f32) + disco_sum
    activated, pullback = jax.vjp(jax.nn.gelu, pre_act)
    output = (field.astype(f32) + activated).astype(bf16)
    grad_pre, = pullback(cotangent.astype(f32))
    grad_pre = grad_pre.astype(bf16)

    def accumulate(carry, block):
        resp = responses(block)
        rows = lax.dynamic_slice_in_dim(grad_pre, (block * LAT_DEV).astype(jnp.int32), LAT_DEV, 0).reshape(-1, C)
        terms = jnp.stack([jnp.dot(resp[tap].reshape(-1, C).T, rows, preferred_element_type=f32) for tap in range(3)])
        return (carry + terms, None)
    grad_disco, _ = lax.scan(accumulate, jnp.zeros((3, C, C), f32), block_ids)
    grad_grid = longitude(grad_pre, synthesis_table).astype(bf16)
    grad_coeffs = project(grad_grid)
    grad_real = grad_coeffs[:, :, 0].reshape(-1, C)
    grad_imag = grad_coeffs[:, :, 1].reshape(-1, C)
    g_real = jnp.dot(real_part.T, grad_real, preferred_element_type=f32) + jnp.dot(imag_part.T, grad_imag, preferred_element_type=f32)
    g_imag = jnp.dot(real_part.T, grad_imag, preferred_element_type=f32) - jnp.dot(imag_part.T, grad_real, preferred_element_type=f32)
    grad_spectral = jnp.stack([g_real, g_imag])
    return (output, grad_spectral, grad_disco)
```

```python
import functools
import math

import jax
import jax.numpy as jnp
from jax import lax
from jax.experimental import pallas as pl
from jax.experimental.pallas import tpu as pltpu
from jax.sharding import PartitionSpec as P

F32 = jnp.float32
BF16 = jnp.bfloat16
LANES = 128
HALF = LANES // 2
GELU_SCALE = math.sqrt(2.0 / math.pi)
GELU_CUBE = 0.044715


def kernel_call(kernel, grid, in_specs, out_specs, out_shape, flops, scratch=(), limit=56):
    leaves = jax.tree.leaves(out_shape)
    size = sum(leaf.size * leaf.dtype.itemsize for leaf in leaves)
    return pl.pallas_call(
        kernel,
        grid=grid,
        in_specs=in_specs,
        out_specs=out_specs,
        out_shape=out_shape,
        scratch_shapes=list(scratch),
        compiler_params=pltpu.CompilerParams(
            dimension_semantics=("arbitrary",) * len(grid), vmem_limit_bytes=limit << 20
        ),
        cost_estimate=pl.CostEstimate(flops=flops, bytes_accessed=3 * size, transcendentals=0),
    )


def low_lanes(rows):
    return lax.broadcasted_iota(jnp.int32, (rows, LANES), 1) < HALF


def swap(value):
    return pltpu.roll(value, HALF, 1)


def exchange(low, first, second):
    return (jnp.where(low, first, swap(second)), jnp.where(low, swap(first), second))


def pack_kernel(field_ref, out_ref):
    low = low_lanes(field_ref.shape[1])
    for tile in range(field_ref.shape[2] // LANES):
        lanes = slice(tile * LANES, (tile + 1) * LANES)
        first, second = exchange(
            low, field_ref[0, :, lanes].astype(F32), field_ref[1, :, lanes].astype(F32)
        )
        out_ref[2 * tile] = first.astype(BF16)
        out_ref[2 * tile + 1] = second.astype(BF16)


def pack(field):
    rows, cols, channels = field.shape
    parts = channels // HALF
    return kernel_call(
        pack_kernel,
        (rows // 2,),
        [pl.BlockSpec((2, cols, channels), lambda i: (i, 0, 0))],
        pl.BlockSpec((parts, cols, LANES), lambda i: (0, 0, i)),
        jax.ShapeDtypeStruct((parts, cols, rows * HALF), BF16),
        0,
    )(field)


def analysis_kernel(pairs, table_ref, slab_ref, weight_ref, out_ref, wide_ref):
    rows = table_ref.shape[0]
    for two in range(pairs // 2):
        lanes = slice(two * 2 * LANES, (two + 1) * 2 * LANES)
        part = jnp.dot(table_ref[...], slab_ref[:, lanes], preferred_element_type=F32)
        part = part * weight_ref[:, lanes]
        wide_ref[pl.ds(2 * two, rows, stride=pairs), :] = part[:, :LANES]
        wide_ref[pl.ds(2 * two + 1, rows, stride=pairs), :] = part[:, LANES:]
    out_ref[...] = wide_ref[...].astype(BF16)


def analysis(table, slabs, weight):
    coefs, nlon = table.shape
    pairs = slabs.shape[1] // LANES
    steps = 4
    rows = coefs // steps
    return kernel_call(
        functools.partial(analysis_kernel, pairs),
        (steps,),
        [
            pl.BlockSpec((rows, nlon), lambda i: (i, 0)),
            pl.BlockSpec(slabs.shape, lambda i: (0, 0)),
            pl.BlockSpec(weight.shape, lambda i: (0, 0)),
        ],
        pl.BlockSpec((rows * pairs, LANES), lambda i: (i, 0)),
        jax.ShapeDtypeStruct((coefs * pairs, LANES), BF16),
        2 * coefs * nlon * slabs.shape[1],
        [pltpu.VMEM((rows * pairs, LANES), F32)],
    )(table, slabs, weight)


def legendre_kernel(slots, pairs, blocks, leg_ref, mask_ref, spec_ref, out_ref, wide_ref, lat_ref, back_ref):
    slot = pl.program_id(0)
    low = low_lanes(blocks)
    rows = 2 * pairs
    piece = 2 * slots * pairs

    @pl.when(slot == 0)
    def _():
        wide_ref[...] = spec_ref[...].astype(F32)

    def taken(part, pair):
        return pl.ds((part * slots + slot) * pairs + pair, blocks, stride=piece)

    for pair in range(pairs):
        even, odd = exchange(low, wide_ref[taken(0, pair), :], wide_ref[taken(1, pair), :])
        lat_ref[pl.ds(2 * pair, blocks, stride=rows), :] = even
        lat_ref[pl.ds(2 * pair + 1, blocks, stride=rows), :] = odd
    leg = leg_ref[0]
    coeffs = lax.dot_general(
        lat_ref[...].astype(BF16), leg, (((0,), (0,)), ((), ())), preferred_element_type=F32
    )
    coeffs = (coeffs * mask_ref[0]).astype(BF16)
    lat_ref[...] = lax.dot_general(
        leg, coeffs, (((1,), (1,)), ((), ())), preferred_element_type=F32
    )
    for pair in range(pairs):
        real, imag = exchange(
            low,
            lat_ref[pl.ds(2 * pair, blocks, stride=rows), :],
            lat_ref[pl.ds(2 * pair + 1, blocks, stride=rows), :],
        )
        back_ref[taken(0, pair), :] = real
        back_ref[taken(1, pair), :] = imag

    @pl.when(slot == slots - 1)
    def _():
        out_ref[...] = back_ref[...].astype(BF16)


def legendre_round_trip(legendre, mask, spectrum, pairs):
    slots, nlat, degrees = legendre.shape
    blocks = nlat // (2 * pairs)
    whole = pl.BlockSpec(spectrum.shape, lambda k: (0, 0))
    return kernel_call(
        functools.partial(legendre_kernel, slots, pairs, blocks),
        (slots,),
        [
            pl.BlockSpec((1, nlat, degrees), lambda k: (k, 0, 0)),
            pl.BlockSpec((1, 1, degrees), lambda k: (k, 0, 0)),
            whole,
        ],
        whole,
        jax.ShapeDtypeStruct(spectrum.shape, BF16),
        4 * slots * nlat * degrees * LANES,
        [
            pltpu.VMEM(spectrum.shape, F32),
            pltpu.VMEM((nlat, LANES), F32),
            pltpu.VMEM(spectrum.shape, F32),
        ],
    )(legendre, mask, spectrum)


def regroup_kernel(pairs, in_ref, out_ref, wide_ref):
    wide_ref[...] = in_ref[...].astype(F32)
    for pair in range(pairs):
        out_ref[pair] = wide_ref[pl.ds(pair, out_ref.shape[1], stride=pairs), :].astype(BF16)


def regroup(rows, pairs):
    coefs = rows.shape[0] // pairs
    return kernel_call(
        functools.partial(regroup_kernel, pairs),
        (1,),
        [pl.BlockSpec(rows.shape, lambda i: (0, 0))],
        pl.BlockSpec((pairs, coefs, LANES), lambda i: (0, 0, 0)),
        jax.ShapeDtypeStruct((pairs, coefs, LANES), BF16),
        0,
        [pltpu.VMEM(rows.shape, F32)],
    )(rows)


def finish_kernel(spec_ref, table_ref, resp_ref, field_ref, cot_ref, weight_ref, out_ref, grad_ref, mix_ref):
    pair = pl.program_id(0)
    parts, _, coefs, _ = spec_ref.shape
    channels = field_ref.shape[2]
    low = low_lanes(coefs)

    @pl.when(pair == 0)
    def _():
        grad_ref[...] = jnp.zeros_like(grad_ref)

    tiles = [
        exchange(low, spec_ref[2 * i, 0].astype(F32), spec_ref[2 * i + 1, 0].astype(F32))
        for i in range(parts // 2)
    ]
    for half in range(2):
        spectrum = jnp.concatenate([tile[half] for tile in tiles], axis=1).astype(BF16)
        for part in range(2):
            mix_ref[:, part * channels : (part + 1) * channels] = jnp.dot(
                table_ref[part], spectrum, preferred_element_type=F32
            ).astype(BF16)
        for tap in range(3):
            mix_ref[:, (2 + tap) * channels : (3 + tap) * channels] = resp_ref[tap, half]
        pre = jnp.dot(mix_ref[...], weight_ref[...], preferred_element_type=F32)
        square = pre * pre
        bend = jnp.tanh(GELU_SCALE * (pre + GELU_CUBE * (square * pre)))
        activated = 0.5 * pre * (1.0 + bend)
        slope = 0.5 * (1.0 + bend) + 0.5 * pre * (1.0 - bend * bend) * (
            GELU_SCALE * (1.0 + 3.0 * GELU_CUBE * square)
        )
        out_ref[half] = (field_ref[half].astype(F32) + activated).astype(BF16)
        grad_pre = (cot_ref[half].astype(F32) * slope).astype(BF16)
        grad_ref[...] += lax.dot_general(
            mix_ref[...], grad_pre, (((0,), (0,)), ((), ())), preferred_element_type=F32
        )


def finish(spectrum, table, responses, field, cotangent, weights):
    rows, cols, channels = field.shape
    parts, pairs, coefs, _ = spectrum.shape
    pixels = pl.BlockSpec((2, cols, channels), lambda i: (i, 0, 0))
    stacked = weights.shape[0]
    return kernel_call(
        finish_kernel,
        (pairs,),
        [
            pl.BlockSpec((parts, 1, coefs, LANES), lambda i: (0, i, 0, 0)),
            pl.BlockSpec(table.shape, lambda i: (0, 0, 0)),
            pl.BlockSpec((3, 2, cols, channels), lambda i: (0, i, 0, 0)),
            pixels,
            pixels,
            pl.BlockSpec(weights.shape, lambda i: (0, 0)),
        ],
        [pixels, pl.BlockSpec((stacked, channels), lambda i: (0, 0))],
        [
            jax.ShapeDtypeStruct(field.shape, BF16),
            jax.ShapeDtypeStruct((stacked, channels), F32),
        ],
        2 * rows * cols * channels * (2 * coefs + 2 * stacked),
        [pltpu.VMEM((cols, stacked), BF16)],
    )(spectrum, table, responses, field, cotangent, weights)


def wave(column, order, shift, nlon):
    quarter = nlon // 4
    phase = (column * order).astype(F32)
    turns = jnp.floor((phase + 0.5) * (1.0 / quarter))
    rest = phase - turns * quarter
    turns = turns + shift.astype(F32)
    turns = turns - 4.0 * jnp.floor(turns * 0.25)
    odd = (turns == 1.0) | (turns == 3.0)
    angle = jnp.where(odd, quarter - rest, rest) * (2.0 * math.pi / nlon)
    square = angle * angle
    total = jnp.full_like(square, 1.0 / math.factorial(12))
    for power in (10, 8, 6, 4, 2, 0):
        total = total * square + (-1.0) ** (power // 2) / math.factorial(power)
    return jnp.where((turns == 1.0) | (turns == 2.0), -total, total)


def disco_responses(field, support_blocks, filter_values):
    rows, cols, _ = field.shape
    lat_pos, size = lax.axis_index("lat"), lax.axis_size("lat")
    up = [(i, i + 1) for i in range(size - 1)]
    down = [(j, i) for i, j in up]
    extended = jnp.concatenate(
        [lax.ppermute(field, "lat", up), field, lax.ppermute(field, "lat", down)], axis=0
    )
    lon = lax.axis_size("lon")
    east = [(i, (i + 1) % lon) for i in range(lon)]
    west = [(j, i) for i, j in east]
    before = lax.ppermute(extended[:, cols - 1 :], "lon", east)
    after = lax.ppermute(extended[:, :1], "lon", west)
    rimmed = jnp.concatenate([before, extended, after], axis=1)
    picks = support_blocks[0] - lat_pos + 1
    onehot = (picks[:, None] == jnp.arange(3, dtype=jnp.int32)[None, :]).astype(F32)
    operator = (
        jnp.einsum("tasb,sq->taqb", filter_values.astype(F32), onehot)
        .reshape(3, rows, 3 * rows)
        .astype(BF16)
    )
    return jnp.stack(
        [
            jnp.einsum(
                "ab,boc->aoc", operator[tap], rimmed[:, tap : tap + cols], preferred_element_type=F32
            ).astype(BF16)
            for tap in range(3)
        ]
    )


def sum_everywhere(terms):
    rows, channels = terms.shape
    lon, lat = lax.axis_size("lon"), lax.axis_size("lat")
    share = rows // lon
    parts = lax.all_to_all(
        terms.astype(BF16).reshape(lon, share, channels), "lon", 0, 0, tiled=True
    )
    partial = jnp.sum(parts.astype(F32), axis=0).astype(BF16)
    step = 8 * pl.cdiv(share, 8 * lat)
    padded = jnp.pad(partial, ((0, lat * step - share), (0, 0))).reshape(lat, step, channels)
    pieces = lax.all_to_all(padded, "lat", 0, 0, tiled=True)
    own = jnp.sum(pieces.astype(F32), axis=0).astype(BF16)
    gathered = lax.all_to_all(
        jnp.broadcast_to(own[None], (lat, step, channels)), "lat", 0, 0, tiled=True
    )
    mine = gathered.reshape(lat * step, channels)[:share]
    everything = lax.all_gather(mine, "lon", tiled=True)
    return everything.astype(F32)


def local(
    field,
    cotangent,
    legendre,
    quad_weight,
    order_slots,
    support_blocks,
    filter_values,
    spectral_weight,
    disco_weight,
):
    rows, cols, channels = field.shape
    lat, lon = lax.axis_size("lat"), lax.axis_size("lon")
    nlon = cols * lon
    slots, nlat, degrees = legendre.shape
    pairs = rows // 2
    lat_pos, lon_pos = lax.axis_index("lat"), lax.axis_index("lon")

    slabs = lax.all_to_all(pack(field), "lon", split_axis=0, concat_axis=0, tiled=True)

    owned = order_slots.reshape(lat, 1, slots)
    row_orders = jnp.broadcast_to(owned, (lat, 2, slots)).reshape(-1)
    row_parts = jnp.broadcast_to(
        jnp.arange(2, dtype=jnp.int32)[None, :, None], (lat, 2, slots)
    ).reshape(-1)
    row_factor = jnp.where(row_orders == 0, 1.0, 2.0).astype(F32)
    columns = jnp.arange(nlon, dtype=jnp.int32)
    analysis_table = wave(columns[None, :], row_orders[:, None], row_parts[:, None], nlon).astype(BF16)
    own_columns = lon_pos * cols + jnp.arange(cols, dtype=jnp.int32)
    quarter_back = jnp.arange(2, dtype=jnp.int32)[:, None, None] * 3
    synthesis_table = (
        row_factor
        * wave(
            own_columns[None, :, None],
            row_orders[None, None, :],
            row_parts[None, None, :] + quarter_back,
            nlon,
        )
    ).astype(BF16)

    lane_weight = jnp.repeat(quad_weight * (1.0 / nlon), HALF)[None, :]
    spectrum = analysis(analysis_table, slabs.reshape(nlon, rows * HALF), lane_weight)
    spectrum = lax.all_to_all(
        spectrum.reshape(lat, -1, LANES), "lat", split_axis=0, concat_axis=0, tiled=True
    ).reshape(spectrum.shape)

    own_orders = lax.dynamic_slice_in_dim(order_slots, lat_pos * slots, slots)
    mask = (jnp.arange(degrees, dtype=jnp.int32)[None, :] >= own_orders[:, None]).astype(F32)
    filtered = legendre_round_trip(legendre, mask[:, None, :], spectrum, pairs)
    filtered = lax.all_to_all(
        filtered.reshape(lat, -1, LANES), "lat", split_axis=0, concat_axis=0, tiled=True
    ).reshape(filtered.shape)
    everywhere = lax.all_gather(regroup(filtered, pairs), "lon")

    responses = disco_responses(field, support_blocks, filter_values)
    weights = jnp.concatenate(
        [
            jnp.stack([spectral_weight[0], -spectral_weight[1]]).reshape(-1, channels),
            disco_weight.reshape(-1, channels),
        ]
    )
    output, terms = finish(everywhere, synthesis_table, responses, field, cotangent, weights)
    sums = sum_everywhere(terms).reshape(5, channels, channels)
    grad_spectral = jnp.stack([sums[0], -sums[1]])
    return (output, grad_spectral, sums[2:])


def solution(mesh):
    placed = (
        P("lat", "lon", None),
        P("lat", "lon", None),
        P("lat", None, None),
        P("lat"),
        P(),
        P("lat", None),
        P(None, "lat", None, None),
        P(),
        P(),
    )
    return jax.shard_map(
        local,
        mesh=mesh,
        in_specs=placed,
        out_specs=(P("lat", "lon", None), P(), P()),
        check_vma=False,
    )
```

```python
import functools
import math

import jax
import jax.numpy as jnp
from jax import lax
from jax.experimental import pallas as pl
from jax.experimental.pallas import tpu as pltpu
from jax.sharding import PartitionSpec as P

F32 = jnp.float32
BF16 = jnp.bfloat16
LANES = 128
HALF = LANES // 2
GELU_SCALE = math.sqrt(2.0 / math.pi)
GELU_CUBE = 0.044715


def kernel_call(kernel, grid, in_specs, out_specs, out_shape, flops, scratch=(), limit=56):
    leaves = jax.tree.leaves(out_shape)
    size = sum(leaf.size * leaf.dtype.itemsize for leaf in leaves)
    return pl.pallas_call(
        kernel,
        grid=grid,
        in_specs=in_specs,
        out_specs=out_specs,
        out_shape=out_shape,
        scratch_shapes=list(scratch),
        compiler_params=pltpu.CompilerParams(
            dimension_semantics=("arbitrary",) * len(grid), vmem_limit_bytes=limit << 20
        ),
        cost_estimate=pl.CostEstimate(flops=flops, bytes_accessed=3 * size, transcendentals=0),
    )


def low_lanes(rows):
    return lax.broadcasted_iota(jnp.int32, (rows, LANES), 1) < HALF


def swap(value):
    return pltpu.roll(value, HALF, 1)


def exchange(low, first, second):
    return (jnp.where(low, first, swap(second)), jnp.where(low, swap(first), second))


def pack_kernel(field_ref, *out_refs):
    low = low_lanes(field_ref.shape[1])
    parts = len(out_refs)
    for ahead, out_ref in enumerate(out_refs):
        quarter = lax.rem(lax.axis_index("lon") + ahead, parts)
        upper = lax.rem(quarter, 2)
        lanes = pl.ds(pl.multiple_of((quarter // 2) * LANES, LANES), LANES)
        first = pltpu.roll(field_ref[0, :, lanes].astype(F32), upper * HALF, 1)
        second = pltpu.roll(field_ref[1, :, lanes].astype(F32), HALF - upper * HALF, 1)
        out_ref[...] = jnp.where(low, first, second).astype(BF16)


def pack(field, start, pairs):
    _, cols, channels = field.shape
    parts = channels // HALF
    return kernel_call(
        pack_kernel,
        (pairs,),
        [pl.BlockSpec((2, cols, channels), lambda i: (start + i, 0, 0))],
        [pl.BlockSpec((cols, LANES), lambda i: (0, i))] * parts,
        [jax.ShapeDtypeStruct((cols, pairs * LANES), BF16)] * parts,
        0,
    )(field)


def project(table_ref, piece_refs, weight_ref):
    total = jnp.dot(table_ref[0], piece_refs[0][...], preferred_element_type=F32)
    for k in range(1, len(piece_refs)):
        total += jnp.dot(table_ref[k], piece_refs[k][...], preferred_element_type=F32)
    return total * weight_ref[...]


def first_analysis_kernel(parts, table_ref, *refs):
    refs[-1][...] = project(table_ref, refs[:parts], refs[parts]).astype(BF16)


def last_analysis_kernel(parts, table_ref, *refs):
    early_ref, out_ref, wide_ref = refs[parts + 1 :]
    half = early_ref.shape[1] // LANES
    rows = early_ref.shape[0]
    late = project(table_ref, refs[:parts], refs[parts])
    for pair in range(half):
        lanes = slice(pair * LANES, (pair + 1) * LANES)
        wide_ref[pl.ds(pair, rows, stride=2 * half), :] = early_ref[:, lanes].astype(F32)
        wide_ref[pl.ds(half + pair, rows, stride=2 * half), :] = late[:, lanes]
    out_ref[...] = wide_ref[...].astype(BF16)


def analysis(table, pieces, weight, early=None):
    parts, coefs, cols = table.shape
    lanes = weight.shape[1]
    steps = 4
    rows = coefs // steps
    whole = pl.BlockSpec((cols, lanes), lambda i: (0, 0))
    block = pl.BlockSpec((rows, lanes), lambda i: (i, 0))
    in_specs = [pl.BlockSpec((parts, rows, cols), lambda i: (0, i, 0))] + [whole] * parts
    in_specs.append(pl.BlockSpec(weight.shape, lambda i: (0, 0)))
    flops = 2 * parts * coefs * cols * lanes
    if early is None:
        return kernel_call(
            functools.partial(first_analysis_kernel, parts),
            (steps,),
            in_specs,
            block,
            jax.ShapeDtypeStruct((coefs, lanes), BF16),
            flops,
        )(table, *pieces, weight)
    pairs = 2 * lanes // LANES
    return kernel_call(
        functools.partial(last_analysis_kernel, parts),
        (steps,),
        in_specs + [block],
        pl.BlockSpec((rows * pairs, LANES), lambda i: (i, 0)),
        jax.ShapeDtypeStruct((coefs * pairs, LANES), BF16),
        flops,
        [pltpu.VMEM((rows * pairs, LANES), F32)],
    )(table, *pieces, weight, early)


def legendre_kernel(slots, pairs, blocks, leg_ref, mask_ref, spec_ref, out_ref, wide_ref, lat_ref, back_ref):
    slot = pl.program_id(0)
    low = low_lanes(blocks)
    rows = 2 * pairs
    piece = 2 * slots * pairs

    @pl.when(slot == 0)
    def _():
        wide_ref[...] = spec_ref[...].astype(F32)

    def taken(part, pair):
        return pl.ds((part * slots + slot) * pairs + pair, blocks, stride=piece)

    for pair in range(pairs):
        even, odd = exchange(low, wide_ref[taken(0, pair), :], wide_ref[taken(1, pair), :])
        lat_ref[pl.ds(2 * pair, blocks, stride=rows), :] = even
        lat_ref[pl.ds(2 * pair + 1, blocks, stride=rows), :] = odd
    leg = leg_ref[0]
    coeffs = lax.dot_general(
        lat_ref[...].astype(BF16), leg, (((0,), (0,)), ((), ())), preferred_element_type=F32
    )
    coeffs = (coeffs * mask_ref[0]).astype(BF16)
    lat_ref[...] = lax.dot_general(
        leg, coeffs, (((1,), (1,)), ((), ())), preferred_element_type=F32
    )
    for pair in range(pairs):
        real, imag = exchange(
            low,
            lat_ref[pl.ds(2 * pair, blocks, stride=rows), :],
            lat_ref[pl.ds(2 * pair + 1, blocks, stride=rows), :],
        )
        back_ref[taken(0, pair), :] = real
        back_ref[taken(1, pair), :] = imag

    @pl.when(slot == slots - 1)
    def _():
        out_ref[...] = back_ref[...].astype(BF16)


def legendre_round_trip(legendre, mask, spectrum, pairs):
    slots, nlat, degrees = legendre.shape
    blocks = nlat // (2 * pairs)
    whole = pl.BlockSpec(spectrum.shape, lambda k: (0, 0))
    return kernel_call(
        functools.partial(legendre_kernel, slots, pairs, blocks),
        (slots,),
        [
            pl.BlockSpec((1, nlat, degrees), lambda k: (k, 0, 0)),
            pl.BlockSpec((1, 1, degrees), lambda k: (k, 0, 0)),
            whole,
        ],
        whole,
        jax.ShapeDtypeStruct(spectrum.shape, BF16),
        4 * slots * nlat * degrees * LANES,
        [
            pltpu.VMEM(spectrum.shape, F32),
            pltpu.VMEM((nlat, LANES), F32),
            pltpu.VMEM(spectrum.shape, F32),
        ],
    )(legendre, mask, spectrum)


def regroup_kernel(in_ref, *refs):
    out_refs, wide_ref = refs[:-1], refs[-1]
    wide_ref[...] = in_ref[...].astype(F32)
    for pair, out_ref in enumerate(out_refs):
        out_ref[...] = wide_ref[pl.ds(pair, out_ref.shape[0], stride=len(out_refs)), :].astype(BF16)


def regroup(rows, pairs):
    coefs = rows.shape[0] // pairs
    steps = 4
    block = coefs // steps
    return kernel_call(
        regroup_kernel,
        (steps,),
        [pl.BlockSpec((block * pairs, LANES), lambda i: (i, 0))],
        [pl.BlockSpec((block, LANES), lambda i: (i, 0))] * pairs,
        [jax.ShapeDtypeStruct((coefs, LANES), BF16)] * pairs,
        0,
        [pltpu.VMEM((block * pairs, LANES), F32)],
    )(rows)


def finish_kernel(count, parts, last, *refs):
    spec_refs, refs = refs[: count * parts], refs[count * parts :]
    table_ref, resp_ref, field_ref, cot_ref, weight_ref = refs[:5]
    sofar_ref = refs[6] if len(refs) > 10 else None
    out_ref, grad_ref, wide_ref, mix_ref, total_ref = refs[-5:]
    step = pl.program_id(0)
    coefs = wide_ref.shape[1]
    channels = field_ref.shape[2]
    low = low_lanes(coefs)

    @pl.when(step == 0)
    def _():
        total_ref[...] = jnp.zeros_like(total_ref) if sofar_ref is None else sofar_ref[...]

    for pair in range(count):

        @pl.when(step == pair)
        def _():
            for behind, spec_ref in enumerate(spec_refs[pair * parts : (pair + 1) * parts]):
                quarter = lax.rem(lax.axis_index("lon") + parts - behind, parts)
                wide_ref[quarter] = spec_ref[...].astype(F32)

    tiles = [exchange(low, wide_ref[2 * i], wide_ref[2 * i + 1]) for i in range(parts // 2)]
    for half in range(2):
        spectrum = jnp.concatenate([tile[half] for tile in tiles], axis=1).astype(BF16)
        for part in range(2):
            mix_ref[:, part * channels : (part + 1) * channels] = jnp.dot(
                table_ref[part], spectrum, preferred_element_type=F32
            ).astype(BF16)
        for tap in range(3):
            mix_ref[:, (2 + tap) * channels : (3 + tap) * channels] = resp_ref[tap, half]
        pre = jnp.dot(mix_ref[...], weight_ref[...], preferred_element_type=F32)
        square = pre * pre
        bend = jnp.tanh(GELU_SCALE * (pre + GELU_CUBE * (square * pre)))
        activated = 0.5 * pre * (1.0 + bend)
        slope = 0.5 * (1.0 + bend) + 0.5 * pre * (1.0 - bend * bend) * (
            GELU_SCALE * (1.0 + 3.0 * GELU_CUBE * square)
        )
        out_ref[half] = (field_ref[half].astype(F32) + activated).astype(BF16)
        grad_pre = (cot_ref[half].astype(F32) * slope).astype(BF16)
        total_ref[...] += lax.dot_general(
            grad_pre, mix_ref[...], (((0,), (0,)), ((), ())), preferred_element_type=F32
        )

    @pl.when(step == count - 1)
    def _():
        if last:
            for part in range(grad_ref.shape[0] // channels):
                span = slice(part * channels, (part + 1) * channels)
                grad_ref[span, :] = total_ref[:, span].T.astype(grad_ref.dtype)
        else:
            grad_ref[...] = total_ref[...]


def finish(spectra, first, table, responses, field, cotangent, weights, output, sofar, last):
    rows, cols, channels = field.shape
    parts, count = len(spectra[0]), len(spectra)
    coefs = spectra[0][0].shape[0]
    pixels = pl.BlockSpec((2, cols, channels), lambda i: (first + i, 0, 0))
    stacked = weights.shape[0]
    whole = pl.BlockSpec((channels, stacked), lambda i: (0, 0))
    turned = (stacked, channels) if last else (channels, stacked)
    call = pl.pallas_call(
        functools.partial(finish_kernel, count, parts, last),
        grid=(count,),
        in_specs=[pl.BlockSpec((coefs, LANES), lambda i: (0, 0))] * (count * parts)
        + [
            pl.BlockSpec(table.shape, lambda i: (0, 0, 0)),
            pl.BlockSpec((3, 2, cols, channels), lambda i: (0, first + i, 0, 0)),
            pixels,
            pixels,
            pl.BlockSpec(weights.shape, lambda i: (0, 0)),
        ]
        + ([] if output is None else [pl.BlockSpec(memory_space=pl.ANY), whole]),
        out_specs=[pixels, pl.BlockSpec(turned, lambda i: (0, 0))],
        out_shape=[
            jax.ShapeDtypeStruct(field.shape, BF16),
            jax.ShapeDtypeStruct(turned, BF16 if last else F32),
        ],
        scratch_shapes=[
            pltpu.VMEM((parts, coefs, LANES), F32),
            pltpu.VMEM((cols, stacked), BF16),
            pltpu.VMEM((channels, stacked), F32),
        ],
        input_output_aliases={} if output is None else {count * parts + 5: 0},
        compiler_params=pltpu.CompilerParams(
            dimension_semantics=("arbitrary",), vmem_limit_bytes=56 << 20
        ),
        cost_estimate=pl.CostEstimate(
            flops=4 * count * 2 * cols * channels * (coefs + stacked),
            bytes_accessed=16 << 20,
            transcendentals=0,
        ),
    )
    pieces = [piece for spectrum in spectra for piece in spectrum]
    earlier = () if output is None else (output, sofar)
    return call(*pieces, table, responses, field, cotangent, weights, *earlier)


def wave(column, order, shift, nlon):
    quarter = nlon // 4
    phase = (column * order).astype(F32)
    turns = jnp.floor((phase + 0.5) * (1.0 / quarter))
    rest = phase - turns * quarter
    turns = turns + shift.astype(F32)
    turns = turns - 4.0 * jnp.floor(turns * 0.25)
    odd = (turns == 1.0) | (turns == 3.0)
    angle = jnp.where(odd, quarter - rest, rest) * (2.0 * math.pi / nlon)
    square = angle * angle
    total = jnp.full_like(square, 1.0 / math.factorial(12))
    for power in (10, 8, 6, 4, 2, 0):
        total = total * square + (-1.0) ** (power // 2) / math.factorial(power)
    return jnp.where((turns == 1.0) | (turns == 2.0), -total, total)


def turn(value, axis, by):
    size = lax.axis_size(axis)
    return lax.ppermute(value, axis, [(i, (i + by) % size) for i in range(size)])


def halo(field):
    size = lax.axis_size("lat")
    up = [(i, i + 1) for i in range(size - 1)]
    down = [(j, i) for i, j in up]
    return (lax.ppermute(field, "lat", up), lax.ppermute(field, "lat", down))


def disco_responses(field, above, below, support_blocks, filter_values):
    rows, cols, _ = field.shape
    lat_pos = lax.axis_index("lat")
    extended = jnp.concatenate([above, field, below], axis=0)
    before = turn(extended[:, cols - 1 :], "lon", 1)
    after = turn(extended[:, :1], "lon", -1)
    rimmed = jnp.concatenate([before, extended, after], axis=1)
    picks = support_blocks[0] - lat_pos + 1
    onehot = (picks[:, None] == jnp.arange(3, dtype=jnp.int32)[None, :]).astype(F32)
    operator = (
        jnp.einsum("tasb,sq->taqb", filter_values.astype(F32), onehot)
        .reshape(3, rows, 3 * rows)
        .astype(BF16)
    )
    return jnp.stack(
        [
            jnp.einsum(
                "ab,boc->aoc", operator[tap], rimmed[:, tap : tap + cols], preferred_element_type=F32
            ).astype(BF16)
            for tap in range(3)
        ]
    )


def swap_with(value, axis, bit):
    return lax.ppermute(value, axis, [(i, i ^ bit) for i in range(lax.axis_size(axis))])


def sum_everywhere(terms):
    rows, channels = terms.shape
    lon, lat = lax.axis_size("lon"), lax.axis_size("lat")
    core = lax.rem(lax.axis_index("lat"), 2)
    half = rows // 2
    kept = lax.dynamic_slice_in_dim(terms, core * half, half)
    given = lax.dynamic_slice_in_dim(terms, (1 - core) * half, half)
    both = (kept.astype(F32) + swap_with(given, "lat", 1).astype(F32)).astype(BF16)
    share = half // lon
    quarters = lax.all_to_all(both.reshape(lon, share, channels), "lon", 0, 0, tiled=True)
    own = jnp.sum(quarters.astype(F32), axis=0).astype(BF16)
    bit = 2
    while bit < lat:
        own = (own.astype(F32) + swap_with(own, "lat", bit).astype(F32)).astype(BF16)
        bit *= 2
    mine = lax.all_to_all(
        jnp.broadcast_to(own[None], (lon, share, channels)), "lon", 0, 0, tiled=True
    ).reshape(half, channels)
    other = swap_with(mine, "lat", 1)
    first = jnp.where(core == 0, mine, other)
    second = jnp.where(core == 0, other, mine)
    return jnp.concatenate([first, second]).astype(F32)


def local(
    field,
    cotangent,
    legendre,
    quad_weight,
    order_slots,
    support_blocks,
    filter_values,
    spectral_weight,
    disco_weight,
):
    rows, cols, channels = field.shape
    lat, lon = lax.axis_size("lat"), lax.axis_size("lon")
    nlon = cols * lon
    slots, nlat, degrees = legendre.shape
    pairs = rows // 2
    lat_pos, lon_pos = lax.axis_index("lat"), lax.axis_index("lon")

    near = pairs // 2
    above, below = halo(field)

    def sent(pieces):
        return [pieces[0]] + [turn(pieces[k], "lon", k) for k in range(1, lon)]

    early_slabs = sent(pack(field, 0, near))
    late_slabs = sent(pack(field, near, near))

    owned = order_slots.reshape(lat, 1, slots)
    row_orders = jnp.broadcast_to(owned, (lat, 2, slots)).reshape(-1)
    row_parts = jnp.broadcast_to(
        jnp.arange(2, dtype=jnp.int32)[None, :, None], (lat, 2, slots)
    ).reshape(-1)
    row_factor = jnp.where(row_orders == 0, 1.0, 2.0).astype(F32)
    starts = lax.rem(lon_pos + lon - jnp.arange(lon, dtype=jnp.int32), lon) * cols
    columns = starts[:, None, None] + jnp.arange(cols, dtype=jnp.int32)[None, None, :]
    analysis_table = wave(
        columns, row_orders[None, :, None], row_parts[None, :, None], nlon
    ).astype(BF16)
    own_columns = lon_pos * cols + jnp.arange(cols, dtype=jnp.int32)
    quarter_back = jnp.arange(2, dtype=jnp.int32)[:, None, None] * 3
    synthesis_table = (
        row_factor
        * wave(
            own_columns[None, :, None],
            row_orders[None, None, :],
            row_parts[None, None, :] + quarter_back,
            nlon,
        )
    ).astype(BF16)

    lane_weight = jnp.repeat(quad_weight * (1.0 / nlon), HALF)[None, :]
    middle = near * LANES
    early = analysis(analysis_table, early_slabs, lane_weight[:, :middle])
    late_slabs, early, above, below = lax.optimization_barrier((late_slabs, early, above, below))
    spectrum = analysis(analysis_table, late_slabs, lane_weight[:, middle:], early)
    spectrum = lax.all_to_all(
        spectrum.reshape(lat, -1, LANES), "lat", split_axis=0, concat_axis=0, tiled=True
    ).reshape(spectrum.shape)
    responses = disco_responses(field, above, below, support_blocks, filter_values)
    spectrum, responses, synthesis_table = lax.optimization_barrier(
        (spectrum, responses, synthesis_table)
    )

    own_orders = lax.dynamic_slice_in_dim(order_slots, lat_pos * slots, slots)
    mask = (jnp.arange(degrees, dtype=jnp.int32)[None, :] >= own_orders[:, None]).astype(F32)
    filtered = legendre_round_trip(legendre, mask[:, None, :], spectrum, pairs)
    filtered = lax.all_to_all(
        filtered.reshape(lat, -1, LANES), "lat", split_axis=0, concat_axis=0, tiled=True
    ).reshape(filtered.shape)
    weights = jnp.concatenate(
        [
            jnp.stack([spectral_weight[0], -spectral_weight[1]]).reshape(-1, channels),
            disco_weight.reshape(-1, channels),
        ]
    )

    def gathered(index, own):
        west, east = turn(own, "lon", 1), turn(own, "lon", -1)
        far = turn(east, "lon", -1) if index % 2 else turn(west, "lon", 1)
        return [own, west, far, east]

    spectra = [gathered(i, own) for i, own in enumerate(regroup(filtered, pairs))]
    output, terms = None, None
    cuts = (0, pairs - 2, pairs - 1, pairs)
    for first, end in zip(cuts[:-1], cuts[1:]):
        output, terms = finish(
            spectra[first:end],
            first,
            synthesis_table,
            responses,
            field,
            cotangent,
            weights,
            output,
            terms,
            end == pairs,
        )
    sums = sum_everywhere(terms).reshape(5, channels, channels)
    grad_spectral = jnp.stack([sums[0], -sums[1]])
    return (output, grad_spectral, sums[2:])


def solution(mesh):
    placed = (
        P("lat", "lon", None),
        P("lat", "lon", None),
        P("lat", None, None),
        P("lat"),
        P(),
        P("lat", None),
        P(None, "lat", None, None),
        P(),
        P(),
    )
    return jax.shard_map(
        local,
        mesh=mesh,
        in_specs=placed,
        out_specs=(P("lat", "lon", None), P(), P()),
        check_vma=False,
    )
```

```python
import functools
import math

import jax
import jax.numpy as jnp
from jax import lax
from jax.experimental import pallas as pl
from jax.experimental.pallas import tpu as pltpu
from jax.sharding import PartitionSpec as P

F32 = jnp.float32
BF16 = jnp.bfloat16
LANES = 128
HALF = LANES // 2
GELU_SCALE = math.sqrt(2.0 / math.pi)
GELU_CUBE = 0.044715


def vmem_call(kernel, operands, out_shape, scratch=(), limit=32, far=()):
    place = pl.BlockSpec(memory_space=pltpu.VMEM)
    places = [pl.BlockSpec(memory_space=pltpu.HBM) if i in far else place for i in range(len(operands))]
    return pl.pallas_call(
        kernel,
        in_specs=places,
        out_specs=jax.tree.map(lambda _: place, out_shape),
        out_shape=out_shape,
        scratch_shapes=list(scratch),
        compiler_params=pltpu.CompilerParams(vmem_limit_bytes=limit << 20),
        cost_estimate=pl.CostEstimate(flops=0, bytes_accessed=1 << 20, transcendentals=0),
    )(*operands)


def low_lanes(rows):
    return lax.broadcasted_iota(jnp.int32, (rows, LANES), 1) < HALF


def swap(value):
    return pltpu.roll(value, HALF, 1)


def exchange(low, first, second):
    return (jnp.where(low, first, swap(second)), jnp.where(low, swap(first), second))


def copy_kernel(value_ref, after_ref, out_ref):
    out_ref[...] = value_ref[...]


def copy_behind(value, after):
    shape = jax.ShapeDtypeStruct(value.shape, value.dtype)
    return vmem_call(copy_kernel, [value, after], shape, far=(1,))


def pack_kernel(field_ref, *out_refs):
    rows, cols, _ = field_ref.shape
    parts = len(out_refs)
    low = low_lanes(cols)
    for ahead, out_ref in enumerate(out_refs):
        quarter = lax.rem(lax.axis_index("lon") + ahead, parts)
        upper = lax.rem(quarter, 2)
        lanes = pl.ds(pl.multiple_of((quarter // 2) * LANES, LANES), LANES)
        for pair in range(rows // 2):
            first = pltpu.roll(field_ref[2 * pair, :, lanes].astype(F32), upper * HALF, 1)
            second = pltpu.roll(field_ref[2 * pair + 1, :, lanes].astype(F32), HALF - upper * HALF, 1)
            out_ref[:, pair * LANES : (pair + 1) * LANES] = jnp.where(low, first, second).astype(BF16)


def pack(field):
    rows, cols, channels = field.shape
    parts = channels // HALF
    return vmem_call(
        pack_kernel, [field], [jax.ShapeDtypeStruct((cols, rows * HALF), BF16)] * parts
    )


def quarter_wave(units, nlon):
    angle = units * (2.0 * math.pi / nlon)
    square = angle * angle
    total = jnp.full_like(square, 1.0 / math.factorial(12))
    for power in (10, 8, 6, 4, 2, 0):
        total = total * square + (-1.0) ** (power // 2) / math.factorial(power)
    return total


def whole_mod_four(value):
    return value - 4.0 * jnp.floor(value * 0.25)


def wave(column, order, ahead, nlon):
    quarter = nlon // 4
    phase = column * order
    turns = jnp.floor((phase + 0.5) * (1.0 / quarter))
    rest = phase - turns * quarter
    cosine = quarter_wave(rest, nlon)
    sine = quarter_wave(quarter - rest, nlon)
    turns = whole_mod_four(turns + ahead)
    odd = (turns == 1.0) | (turns == 3.0)
    here = jnp.where(odd, sine, cosine)
    further = jnp.where(odd, cosine, sine)
    here = jnp.where((turns == 1.0) | (turns == 2.0), -here, here)
    further = jnp.where(turns < 1.5, -further, further)
    return (here, further)


def advance(here, further, turns):
    turns = whole_mod_four(turns)
    even = (turns == 0.0).astype(F32) - (turns == 2.0).astype(F32)
    odd = (turns == 1.0).astype(F32) - (turns == 3.0).astype(F32)
    return even * here + odd * further


def table_kernel(down_ref, across_ref, after_ref, analysis_ref, synthesis_ref):
    parts, rows, cols = analysis_ref.shape
    nlon = parts * cols
    place = lax.axis_index("lon")
    order, part = down_ref[:, 0:1], down_ref[:, 1:2]
    column = lax.broadcasted_iota(jnp.int32, (rows, cols), 1).astype(F32)
    here, further = wave(column, order, part, nlon)
    for k in range(parts):
        slab = lax.rem(place + parts - k, parts).astype(F32)
        analysis_ref[k] = advance(here, further, slab * order).astype(BF16)
    order, part = across_ref[0:1, :], across_ref[1:2, :]
    column = lax.broadcasted_iota(jnp.int32, (cols, rows), 0).astype(F32)
    here, further = wave(column, order, part, nlon)
    factor = jnp.where(order == 0.0, 1.0, 2.0)
    turns = place.astype(F32) * order
    for back in range(2):
        synthesis_ref[back] = (factor * advance(here, further, turns + back)).astype(BF16)


def fourier_tables(row_orders, row_parts, parts, after):
    coefs, cols = row_orders.shape[0], after.shape[1]
    both = jnp.stack([row_orders, row_parts]).astype(F32)
    return vmem_call(
        table_kernel,
        [both.T, both, after],
        [
            jax.ShapeDtypeStruct((parts, coefs, cols), BF16),
            jax.ShapeDtypeStruct((2, cols, coefs), BF16),
        ],
        far=(2,),
    )


def analysis_kernel(parts, table_ref, *refs):
    weight_ref, out_ref, wide_ref = refs[parts:]
    rows = table_ref.shape[1]
    total = jnp.dot(table_ref[0], refs[0][...], preferred_element_type=F32)
    for k in range(1, parts):
        total += jnp.dot(table_ref[k], refs[k][...], preferred_element_type=F32)
    total = total * weight_ref[...]
    pairs = total.shape[1] // LANES
    for pair in range(pairs):
        wide_ref[pl.ds(pair, rows, stride=pairs), :] = total[:, pair * LANES : (pair + 1) * LANES]
    out_ref[...] = wide_ref[...].astype(BF16)


def analysis(table, pieces, weight):
    parts, coefs, _ = table.shape
    shape = (coefs * weight.shape[1] // LANES, LANES)
    return vmem_call(
        functools.partial(analysis_kernel, parts),
        [table, *pieces, weight],
        jax.ShapeDtypeStruct(shape, BF16),
        [pltpu.VMEM(shape, F32)],
    )


def legendre_kernel(pairs, far_ref, mask_ref, spec_ref, out_ref, leg_ref, wide_ref, lat_ref, back_ref, sems):
    slots, nlat, _ = leg_ref.shape
    loads = [pltpu.make_async_copy(far_ref.at[k], leg_ref.at[k], sems.at[k]) for k in range(slots)]
    for load in loads:
        load.start()
    rows = 2 * pairs
    blocks = nlat // rows
    piece = 2 * slots * pairs
    low = low_lanes(blocks)
    wide_ref[...] = spec_ref[...].astype(F32)
    for slot in range(slots):
        lat = lat_ref.at[slot]

        def taken(part, pair):
            return pl.ds((part * slots + slot) * pairs + pair, blocks, stride=piece)

        for pair in range(pairs):
            even, odd = exchange(low, wide_ref[taken(0, pair), :], wide_ref[taken(1, pair), :])
            lat[pl.ds(2 * pair, blocks, stride=rows), :] = even
            lat[pl.ds(2 * pair + 1, blocks, stride=rows), :] = odd
        loads[slot].wait()
        leg = leg_ref[slot]
        coeffs = lax.dot_general(
            lat[...].astype(BF16), leg, (((0,), (0,)), ((), ())), preferred_element_type=F32
        )
        coeffs = (coeffs * mask_ref[slot]).astype(BF16)
        lat[...] = lax.dot_general(leg, coeffs, (((1,), (1,)), ((), ())), preferred_element_type=F32)
        for pair in range(pairs):
            real, imag = exchange(
                low,
                lat[pl.ds(2 * pair, blocks, stride=rows), :],
                lat[pl.ds(2 * pair + 1, blocks, stride=rows), :],
            )
            back_ref[taken(0, pair), :] = real
            back_ref[taken(1, pair), :] = imag
    out_ref[...] = back_ref[...].astype(BF16)


def legendre_round_trip(legendre, mask, spectrum, pairs):
    slots, nlat, _ = legendre.shape
    return vmem_call(
        functools.partial(legendre_kernel, pairs),
        [legendre, mask, spectrum],
        jax.ShapeDtypeStruct(spectrum.shape, BF16),
        [
            pltpu.VMEM(legendre.shape, BF16),
            pltpu.VMEM(spectrum.shape, F32),
            pltpu.VMEM((slots, nlat, LANES), F32),
            pltpu.VMEM(spectrum.shape, F32),
            pltpu.SemaphoreType.DMA((slots,)),
        ],
        far=(0,),
    )


def finish_kernel(
    own_ref,
    west_ref,
    far_west_ref,
    far_east_ref,
    east_ref,
    table_ref,
    resp_ref,
    disco_ref,
    field_ref,
    cot_ref,
    weight_ref,
    out_ref,
    grad_ref,
    wide_ref,
    mix_ref,
    total_ref,
):
    pairs, _, channels = field_ref.shape
    parts, rows, _ = wide_ref.shape
    coefs = rows // pairs
    low = low_lanes(coefs)
    place = lax.axis_index("lon")
    wide_ref[place] = own_ref[...].astype(F32)
    wide_ref[lax.rem(place + parts - 1, parts)] = west_ref[...].astype(F32)
    wide_ref[lax.rem(place + 1, parts)] = east_ref[...].astype(F32)
    across = lax.rem(place + 2, parts)
    middle = rows // 2
    wide_ref[across, :middle] = far_west_ref[...].astype(F32)
    wide_ref[across, middle:] = far_east_ref[...].astype(F32)
    for pair in range(pairs):
        mix = mix_ref.at[pair]
        held = [wide_ref[part, pl.ds(pair, coefs, stride=pairs), :] for part in range(parts)]
        tiles = [exchange(low, held[2 * i], held[2 * i + 1]) for i in range(parts // 2)]
        spectrum = jnp.concatenate([tile[half] for half in range(2) for tile in tiles], axis=1)
        spectrum = spectrum.astype(BF16)
        for part in range(2):
            grid = jnp.dot(table_ref[part], spectrum, preferred_element_type=F32)
            grid = jnp.concatenate([grid[:, :channels], grid[:, channels:]], axis=0)
            mix[:, part * channels : (part + 1) * channels] = grid.astype(BF16)
        pre = jnp.dot(mix[...], weight_ref[...], preferred_element_type=F32) + disco_ref[pair]
        square = pre * pre
        bend = jnp.tanh(GELU_SCALE * (pre + GELU_CUBE * (square * pre)))
        activated = 0.5 * pre * (1.0 + bend)
        slope = 0.5 * (1.0 + bend) + 0.5 * pre * (1.0 - bend * bend) * (
            GELU_SCALE * (1.0 + 3.0 * GELU_CUBE * square)
        )
        out_ref[pair] = (field_ref[pair].astype(F32) + activated).astype(BF16)
        grad_pre = (cot_ref[pair].astype(F32) * slope).astype(BF16)
        start = 0
        for values in [mix[...]] + [resp_ref[tap, pair] for tap in range(resp_ref.shape[0])]:
            term = lax.dot_general(
                grad_pre, values, (((0,), (0,)), ((), ())), preferred_element_type=F32
            )
            span = slice(start, start + values.shape[1])
            start = span.stop
            if pair == 0:
                total_ref[:, span] = term
            else:
                total_ref[:, span] += term
    for part in range(grad_ref.shape[0] // channels):
        span = slice(part * channels, (part + 1) * channels)
        grad_ref[span, :] = total_ref[:, span].T.astype(BF16)


def finish(spectra, table, responses, disco_sum, field, cotangent, weight):
    rows, cols, channels = field.shape
    pairs = rows // 2
    grouped = (pairs, 2 * cols, channels)
    taps = responses.shape[0]
    stacked = weight.shape[0] + taps * channels
    output, grads = vmem_call(
        finish_kernel,
        [
            *spectra,
            table,
            responses.reshape(taps, *grouped),
            disco_sum.reshape(grouped),
            field.reshape(grouped),
            cotangent.reshape(grouped),
            weight,
        ],
        [jax.ShapeDtypeStruct(grouped, BF16), jax.ShapeDtypeStruct((stacked, channels), BF16)],
        [
            pltpu.VMEM((channels // HALF, spectra[0].shape[0], LANES), F32),
            pltpu.VMEM((pairs, 2 * cols, weight.shape[0]), BF16),
            pltpu.VMEM((channels, stacked), F32),
        ],
    )
    return output.reshape(field.shape), grads


def turn(value, axis, by):
    size = lax.axis_size(axis)
    return lax.ppermute(value, axis, [(i, (i + by) % size) for i in range(size)])


def halo(field):
    size = lax.axis_size("lat")
    up = [(i, i + 1) for i in range(size - 1)]
    down = [(j, i) for i, j in up]
    return (lax.ppermute(field, "lat", up), lax.ppermute(field, "lat", down))


def disco_responses(above, field, below, support_blocks, filter_values):
    rows, cols, _ = field.shape
    lat_pos = lax.axis_index("lat")
    blocks = jnp.concatenate([above, field, below], axis=0)
    picks = support_blocks[0] - lat_pos + 1
    onehot = (picks[:, None] == jnp.arange(3, dtype=jnp.int32)[None, :]).astype(F32)
    operator = (
        jnp.einsum("tasb,sq->taqb", filter_values.astype(F32), onehot)
        .reshape(3, rows, 3 * rows)
        .astype(BF16)
    )
    here, level, there = (
        jnp.einsum("ab,boc->aoc", operator[tap], blocks, preferred_element_type=F32).astype(BF16)
        for tap in range(3)
    )
    first = turn(here[:, cols - 1 :], "lon", 1)
    last = turn(there[:, :1], "lon", -1)
    return jnp.stack(
        [
            jnp.concatenate([first, here[:, : cols - 1]], axis=1),
            level,
            jnp.concatenate([there[:, 1:], last], axis=1),
        ]
    )


def sum_everywhere(terms):
    rows, channels = terms.shape
    lon, lat = lax.axis_size("lon"), lax.axis_size("lat")
    side = 8 if lat % 8 == 0 else lat
    count = side * lon
    planes = [list(range(z * count, (z + 1) * count)) for z in range(lat // side)]
    columns = [list(range(i, lat, side)) for i in range(side)]
    share = rows // count
    pieces = lax.all_to_all(
        terms.reshape(count, share, channels),
        ("lat", "lon"),
        0,
        0,
        tiled=True,
        axis_index_groups=planes,
    )
    own = jnp.sum(pieces.astype(F32), axis=0).astype(BF16)
    others = lax.all_to_all(
        jnp.broadcast_to(own[None], (lat // side, share, channels)),
        "lat",
        0,
        0,
        tiled=True,
        axis_index_groups=columns,
    )
    total = jnp.sum(others.astype(F32), axis=0).astype(BF16)
    everything = lax.all_to_all(
        jnp.broadcast_to(total[None], (count, share, channels)),
        ("lat", "lon"),
        0,
        0,
        tiled=True,
        axis_index_groups=planes,
    )
    return everything.reshape(rows, channels).astype(F32)


def local(
    field,
    cotangent,
    legendre,
    quad_weight,
    order_slots,
    support_blocks,
    filter_values,
    spectral_weight,
    disco_weight,
):
    rows, cols, channels = field.shape
    lat, lon = lax.axis_size("lat"), lax.axis_size("lon")
    nlon = cols * lon
    slots, nlat, degrees = legendre.shape
    pairs = rows // 2
    lat_pos, lon_pos = lax.axis_index("lat"), lax.axis_index("lon")

    pieces = pack(field)
    slabs = [pieces[0]] + [turn(pieces[k], "lon", k) for k in range(1, lon)]

    row_orders = jnp.broadcast_to(order_slots.reshape(lat, 1, slots), (lat, 2, slots)).reshape(-1)
    row_parts = jnp.broadcast_to(
        jnp.arange(2, dtype=jnp.int32)[None, :, None], (lat, 2, slots)
    ).reshape(-1)
    copied = copy_behind(field, pieces[0])
    above, below = halo(copied)
    analysis_table, synthesis_table = fourier_tables(row_orders, row_parts, lon, copied)
    lane_weight = jnp.repeat(quad_weight * (1.0 / nlon), HALF)[None, :]
    spectrum = analysis(analysis_table, slabs, lane_weight)
    own_orders = lax.dynamic_slice_in_dim(order_slots, lat_pos * slots, slots)
    mask = (jnp.arange(degrees, dtype=jnp.int32)[None, :] >= own_orders[:, None]).astype(F32)
    spectrum, above, below, mask = lax.optimization_barrier((spectrum, above, below, mask))
    spectrum = lax.all_to_all(
        spectrum.reshape(lat, -1, LANES), "lat", split_axis=0, concat_axis=0, tiled=True
    ).reshape(spectrum.shape)
    filtered = legendre_round_trip(legendre, mask[:, None, :], spectrum, pairs)
    filtered = lax.all_to_all(
        filtered.reshape(lat, -1, LANES), "lat", split_axis=0, concat_axis=0, tiled=True
    ).reshape(filtered.shape)
    filtered, above, below = lax.optimization_barrier((filtered, above, below))
    west, east = turn(filtered, "lon", 1), turn(filtered, "lon", -1)
    middle = filtered.shape[0] // 2
    far_west, far_east = turn(west[:middle], "lon", 1), turn(east[middle:], "lon", -1)
    responses = disco_responses(above, field, below, support_blocks, filter_values)
    disco_sum = sum(
        jnp.dot(responses[tap].reshape(-1, channels), disco_weight[tap], preferred_element_type=F32)
        for tap in range(responses.shape[0])
    )

    output, terms = finish(
        (filtered, west, far_west, far_east, east),
        synthesis_table,
        responses,
        disco_sum,
        field,
        cotangent,
        spectral_weight.reshape(-1, channels),
    )
    sums = sum_everywhere(terms)
    spectral = spectral_weight.shape[0] * channels
    return (
        output,
        sums[:spectral].reshape(spectral_weight.shape),
        sums[spectral:].reshape(disco_weight.shape),
    )


def solution(mesh):
    placed = (
        P("lat", "lon", None),
        P("lat", "lon", None),
        P("lat", None, None),
        P("lat"),
        P(),
        P("lat", None),
        P(None, "lat", None, None),
        P(),
        P(),
    )
    return jax.shard_map(
        local,
        mesh=mesh,
        in_specs=placed,
        out_specs=(P("lat", "lon", None), P(), P()),
        check_vma=False,
    )
```

```python
import functools
import math

import jax
import jax.numpy as jnp
from jax import lax
from jax.experimental import pallas as pl
from jax.experimental.pallas import tpu as pltpu
from jax.sharding import PartitionSpec as P

F32 = jnp.float32
BF16 = jnp.bfloat16
LANES = 128
HALF = LANES // 2
GELU_SCALE = math.sqrt(2.0 / math.pi)
GELU_CUBE = 0.044715


def vmem_call(kernel, operands, out_shape, scratch=(), limit=32, far=()):
    place = pl.BlockSpec(memory_space=pltpu.VMEM)
    places = [pl.BlockSpec(memory_space=pl.ANY) if i in far else place for i in range(len(operands))]
    return pl.pallas_call(
        kernel,
        in_specs=places,
        out_specs=jax.tree.map(lambda _: place, out_shape),
        out_shape=out_shape,
        scratch_shapes=list(scratch),
        compiler_params=pltpu.CompilerParams(vmem_limit_bytes=limit << 20),
        cost_estimate=pl.CostEstimate(flops=0, bytes_accessed=1 << 20, transcendentals=0),
    )(*operands)


def low_lanes(rows):
    return lax.broadcasted_iota(jnp.int32, (rows, LANES), 1) < HALF


def swap(value):
    return pltpu.roll(value, HALF, 1)


def exchange(low, first, second):
    return (jnp.where(low, first, swap(second)), jnp.where(low, swap(first), second))


def copy_kernel(value_ref, after_ref, out_ref):
    out_ref[...] = value_ref[...]


def copy_behind(value, after):
    shape = jax.ShapeDtypeStruct(value.shape, value.dtype)
    return vmem_call(copy_kernel, [value, after], shape, far=(1,))


def pack_kernel(field_ref, *out_refs):
    rows, cols, _ = field_ref.shape
    parts = len(out_refs)
    low = low_lanes(cols)
    for ahead, out_ref in enumerate(out_refs):
        quarter = lax.rem(lax.axis_index("lon") + ahead, parts)
        upper = lax.rem(quarter, 2)
        lanes = pl.ds(pl.multiple_of((quarter // 2) * LANES, LANES), LANES)
        for pair in range(rows // 2):
            first = pltpu.roll(field_ref[2 * pair, :, lanes].astype(F32), upper * HALF, 1)
            second = pltpu.roll(field_ref[2 * pair + 1, :, lanes].astype(F32), HALF - upper * HALF, 1)
            out_ref[:, pair * LANES : (pair + 1) * LANES] = jnp.where(low, first, second).astype(BF16)


def pack(field):
    rows, cols, channels = field.shape
    parts = channels // HALF
    return vmem_call(
        pack_kernel, [field], [jax.ShapeDtypeStruct((cols, rows * HALF), BF16)] * parts
    )


def quarter_wave(units, nlon):
    angle = units * (2.0 * math.pi / nlon)
    square = angle * angle
    total = jnp.full_like(square, 1.0 / math.factorial(12))
    for power in (10, 8, 6, 4, 2, 0):
        total = total * square + (-1.0) ** (power // 2) / math.factorial(power)
    return total


def whole_mod_four(value):
    return value - 4.0 * jnp.floor(value * 0.25)


def wave(column, order, ahead, nlon):
    quarter = nlon // 4
    phase = column * order
    turns = jnp.floor((phase + 0.5) * (1.0 / quarter))
    rest = phase - turns * quarter
    cosine = quarter_wave(rest, nlon)
    sine = quarter_wave(quarter - rest, nlon)
    turns = whole_mod_four(turns + ahead)
    odd = (turns == 1.0) | (turns == 3.0)
    here = jnp.where(odd, sine, cosine)
    further = jnp.where(odd, cosine, sine)
    here = jnp.where((turns == 1.0) | (turns == 2.0), -here, here)
    further = jnp.where(turns < 1.5, -further, further)
    return (here, further)


def advance(here, further, turns):
    turns = whole_mod_four(turns)
    even = (turns == 0.0).astype(F32) - (turns == 2.0).astype(F32)
    odd = (turns == 1.0).astype(F32) - (turns == 3.0).astype(F32)
    return even * here + odd * further


def table_kernel(down_ref, across_ref, after_ref, analysis_ref, synthesis_ref):
    parts, rows, cols = analysis_ref.shape
    nlon = parts * cols
    place = lax.axis_index("lon")
    order, part = down_ref[:, 0:1], down_ref[:, 1:2]
    column = lax.broadcasted_iota(jnp.int32, (rows, cols), 1).astype(F32)
    here, further = wave(column, order, part, nlon)
    for k in range(parts):
        slab = lax.rem(place + parts - k, parts).astype(F32)
        analysis_ref[k] = advance(here, further, slab * order).astype(BF16)
    order, part = across_ref[0:1, :], across_ref[1:2, :]
    column = lax.broadcasted_iota(jnp.int32, (cols, rows), 0).astype(F32)
    here, further = wave(column, order, part, nlon)
    factor = jnp.where(order == 0.0, 1.0, 2.0)
    turns = place.astype(F32) * order
    for back in range(2):
        synthesis_ref[back] = (factor * advance(here, further, turns + back)).astype(BF16)


def fourier_tables(row_orders, row_parts, parts, after):
    coefs, cols = row_orders.shape[0], after.shape[1]
    both = jnp.stack([row_orders, row_parts]).astype(F32)
    return vmem_call(
        table_kernel,
        [both.T, both, after],
        [
            jax.ShapeDtypeStruct((parts, coefs, cols), BF16),
            jax.ShapeDtypeStruct((2, cols, coefs), BF16),
        ],
        far=(2,),
    )


def analysis_kernel(parts, table_ref, *refs):
    weight_ref, out_ref, wide_ref = refs[parts:]
    rows = table_ref.shape[1]
    total = jnp.dot(table_ref[0], refs[0][...], preferred_element_type=F32)
    for k in range(1, parts):
        total += jnp.dot(table_ref[k], refs[k][...], preferred_element_type=F32)
    total = total * weight_ref[...]
    pairs = total.shape[1] // LANES
    for pair in range(pairs):
        wide_ref[pl.ds(pair, rows, stride=pairs), :] = total[:, pair * LANES : (pair + 1) * LANES]
    out_ref[...] = wide_ref[...].astype(BF16)


def analysis(table, pieces, weight):
    parts, coefs, _ = table.shape
    shape = (coefs * weight.shape[1] // LANES, LANES)
    return vmem_call(
        functools.partial(analysis_kernel, parts),
        [table, *pieces, weight],
        jax.ShapeDtypeStruct(shape, BF16),
        [pltpu.VMEM(shape, F32)],
    )


def legendre_kernel(pairs, leg_ref, mask_ref, spec_ref, out_ref, wide_ref, lat_ref, back_ref):
    slots, nlat, _ = leg_ref.shape
    rows = 2 * pairs
    blocks = nlat // rows
    piece = 2 * slots * pairs
    low = low_lanes(blocks)
    wide_ref[...] = spec_ref[...].astype(F32)
    for slot in range(slots):
        lat = lat_ref.at[slot]

        def taken(part, pair):
            return pl.ds((part * slots + slot) * pairs + pair, blocks, stride=piece)

        for pair in range(pairs):
            even, odd = exchange(low, wide_ref[taken(0, pair), :], wide_ref[taken(1, pair), :])
            lat[pl.ds(2 * pair, blocks, stride=rows), :] = even
            lat[pl.ds(2 * pair + 1, blocks, stride=rows), :] = odd
        leg = leg_ref[slot]
        coeffs = lax.dot_general(
            lat[...].astype(BF16), leg, (((0,), (0,)), ((), ())), preferred_element_type=F32
        )
        coeffs = (coeffs * mask_ref[slot]).astype(BF16)
        lat[...] = lax.dot_general(leg, coeffs, (((1,), (1,)), ((), ())), preferred_element_type=F32)
        for pair in range(pairs):
            real, imag = exchange(
                low,
                lat[pl.ds(2 * pair, blocks, stride=rows), :],
                lat[pl.ds(2 * pair + 1, blocks, stride=rows), :],
            )
            back_ref[taken(0, pair), :] = real
            back_ref[taken(1, pair), :] = imag
    out_ref[...] = back_ref[...].astype(BF16)


def legendre_round_trip(legendre, mask, spectrum, pairs):
    slots, nlat, _ = legendre.shape
    return vmem_call(
        functools.partial(legendre_kernel, pairs),
        [legendre, mask, spectrum],
        jax.ShapeDtypeStruct(spectrum.shape, BF16),
        [
            pltpu.VMEM(spectrum.shape, F32),
            pltpu.VMEM((slots, nlat, LANES), F32),
            pltpu.VMEM(spectrum.shape, F32),
        ],
    )


def synthesis(table_ref, wide_ref, pairs):
    coefs = table_ref.shape[2]
    held = [wide_ref[pl.ds(pair, coefs, stride=pairs), :] for pair in range(pairs)]
    spectrum = jnp.concatenate(held, axis=1).astype(BF16)
    return [
        jnp.dot(table_ref[part], spectrum, preferred_element_type=F32)
        for part in range(table_ref.shape[0])
    ]


def synthesis_kernel(table_ref, *refs):
    wide_ref = refs[-1]
    count = len(refs) // 2
    for in_ref, out_ref in zip(refs[:count], refs[count:-1]):
        wide_ref[...] = in_ref[...].astype(F32)
        pairs = out_ref.shape[1]
        for part, grid in enumerate(synthesis(table_ref, wide_ref, pairs)):
            for pair in range(pairs):
                out_ref[part, pair] = grid[:, pair * LANES : (pair + 1) * LANES].astype(BF16)


def synthesize(table, *spectra):
    parts, cols, coefs = table.shape
    rows = spectra[0].shape[0]
    shape = jax.ShapeDtypeStruct((parts, rows // coefs, cols, LANES), BF16)
    return vmem_call(
        synthesis_kernel,
        [table, *spectra],
        [shape] * len(spectra),
        [pltpu.VMEM((rows, LANES), F32)],
    )


def finish_kernel(
    own_ref,
    west_ref,
    east_ref,
    far_west_ref,
    far_east_ref,
    table_ref,
    resp_ref,
    disco_ref,
    field_ref,
    cot_ref,
    weight_ref,
    out_ref,
    grad_ref,
    wide_ref,
    mix_ref,
    total_ref,
):
    pairs, _, channels = field_ref.shape
    cols = table_ref.shape[1]
    middle = far_west_ref.shape[0]
    low = low_lanes(cols)
    place = lax.axis_index("lon")
    odd = lax.rem(place, 2) == 1
    near = place // 2
    wide_ref[:middle] = far_west_ref[...].astype(F32)
    wide_ref[middle:] = far_east_ref[...].astype(F32)
    far_grid = synthesis(table_ref, wide_ref, pairs)
    for pair in range(pairs):
        mix = mix_ref.at[pair]
        for part in range(2):
            own, west, east = (
                ref[part, pair].astype(F32) for ref in (own_ref, west_ref, east_ref)
            )
            far = far_grid[part][:, pair * LANES : (pair + 1) * LANES]
            tiles = [
                (near, jnp.where(odd, west, own), jnp.where(odd, own, east)),
                (1 - near, jnp.where(odd, east, far), jnp.where(odd, far, west)),
            ]
            for tile, first, second in tiles:
                start = pl.multiple_of(part * channels + tile * LANES, LANES)
                grid = jnp.concatenate(exchange(low, first, second), axis=0).astype(BF16)
                mix[:, pl.ds(start, LANES)] = grid
        pre = jnp.dot(mix[...], weight_ref[...], preferred_element_type=F32) + disco_ref[pair]
        square = pre * pre
        bend = jnp.tanh(GELU_SCALE * (pre + GELU_CUBE * (square * pre)))
        activated = 0.5 * pre * (1.0 + bend)
        slope = 0.5 * (1.0 + bend) + 0.5 * pre * (1.0 - bend * bend) * (
            GELU_SCALE * (1.0 + 3.0 * GELU_CUBE * square)
        )
        out_ref[pair] = (field_ref[pair].astype(F32) + activated).astype(BF16)
        grad_pre = (cot_ref[pair].astype(F32) * slope).astype(BF16)
        start = 0
        for values in [mix[...]] + [resp_ref[tap, pair] for tap in range(resp_ref.shape[0])]:
            term = lax.dot_general(
                grad_pre, values, (((0,), (0,)), ((), ())), preferred_element_type=F32
            )
            span = slice(start, start + values.shape[1])
            start = span.stop
            if pair == 0:
                total_ref[:, span] = term
            else:
                total_ref[:, span] += term
    for part in range(grad_ref.shape[0] // channels):
        span = slice(part * channels, (part + 1) * channels)
        grad_ref[span, :] = total_ref[:, span].T.astype(BF16)


def finish(spectra, table, responses, disco_sum, field, cotangent, weight):
    rows, cols, channels = field.shape
    pairs = rows // 2
    grouped = (pairs, 2 * cols, channels)
    taps = responses.shape[0]
    stacked = weight.shape[0] + taps * channels
    output, grads = vmem_call(
        finish_kernel,
        [
            *spectra,
            table,
            responses.reshape(taps, *grouped),
            disco_sum.reshape(grouped),
            field.reshape(grouped),
            cotangent.reshape(grouped),
            weight,
        ],
        [jax.ShapeDtypeStruct(grouped, BF16), jax.ShapeDtypeStruct((stacked, channels), BF16)],
        [
            pltpu.VMEM((pairs * table.shape[2], LANES), F32),
            pltpu.VMEM((pairs, 2 * cols, weight.shape[0]), BF16),
            pltpu.VMEM((channels, stacked), F32),
        ],
    )
    return output.reshape(field.shape), grads


def turn(value, axis, by):
    size = lax.axis_size(axis)
    return lax.ppermute(value, axis, [(i, (i + by) % size) for i in range(size)])


def disco_responses(above, field, below, support_blocks, filter_values):
    rows, cols, _ = field.shape
    lat_pos = lax.axis_index("lat")
    blocks = jnp.concatenate([above, field, below], axis=0)
    picks = support_blocks[0] - lat_pos + 1
    onehot = (picks[:, None] == jnp.arange(3, dtype=jnp.int32)[None, :]).astype(F32)
    operator = (
        jnp.einsum("tasb,sq->taqb", filter_values.astype(F32), onehot)
        .reshape(3, rows, 3 * rows)
        .astype(BF16)
    )
    here, level, there = (
        jnp.einsum("ab,boc->aoc", operator[tap], blocks, preferred_element_type=F32).astype(BF16)
        for tap in range(3)
    )
    first = turn(here[:, cols - 1 :], "lon", 1)
    last = turn(there[:, :1], "lon", -1)
    return jnp.stack(
        [
            jnp.concatenate([first, here[:, : cols - 1]], axis=1),
            level,
            jnp.concatenate([there[:, 1:], last], axis=1),
        ]
    )


def sum_everywhere(terms):
    rows, channels = terms.shape
    lon, lat = lax.axis_size("lon"), lax.axis_size("lat")
    side = 8 if lat % 8 == 0 else lat
    count = side * lon
    planes = [list(range(z * count, (z + 1) * count)) for z in range(lat // side)]
    columns = [list(range(i, lat, side)) for i in range(side)]
    share = rows // count
    pieces = lax.all_to_all(
        terms.reshape(count, share, channels),
        ("lat", "lon"),
        0,
        0,
        tiled=True,
        axis_index_groups=planes,
    )
    own = jnp.sum(pieces.astype(F32), axis=0).astype(BF16)
    others = lax.all_to_all(
        jnp.broadcast_to(own[None], (lat // side, share, channels)),
        "lat",
        0,
        0,
        tiled=True,
        axis_index_groups=columns,
    )
    total = jnp.sum(others.astype(F32), axis=0).astype(BF16)
    everything = lax.all_to_all(
        jnp.broadcast_to(total[None], (count, share, channels)),
        ("lat", "lon"),
        0,
        0,
        tiled=True,
        axis_index_groups=planes,
    )
    return everything.reshape(rows, channels).astype(F32)


def local(
    field,
    cotangent,
    legendre,
    quad_weight,
    order_slots,
    support_blocks,
    filter_values,
    spectral_weight,
    disco_weight,
):
    rows, cols, channels = field.shape
    lat, lon = lax.axis_size("lat"), lax.axis_size("lon")
    nlon = cols * lon
    slots, nlat, degrees = legendre.shape
    pairs = rows // 2
    lat_pos, lon_pos = lax.axis_index("lat"), lax.axis_index("lon")

    pieces = pack(field)
    slabs = [pieces[0]] + [turn(pieces[k], "lon", k) for k in range(1, lon)]

    row_orders = jnp.broadcast_to(order_slots.reshape(lat, 1, slots), (lat, 2, slots)).reshape(-1)
    row_parts = jnp.broadcast_to(
        jnp.arange(2, dtype=jnp.int32)[None, :, None], (lat, 2, slots)
    ).reshape(-1)
    copied = copy_behind(field, pieces[0])
    above, below = turn(copied, "lat", 1), turn(copied, "lat", -1)
    analysis_table, synthesis_table = fourier_tables(row_orders, row_parts, lon, copied)
    lane_weight = jnp.repeat(quad_weight * (1.0 / nlon), HALF)[None, :]
    spectrum = analysis(analysis_table, slabs, lane_weight)
    own_orders = lax.dynamic_slice_in_dim(order_slots, lat_pos * slots, slots)
    mask = (jnp.arange(degrees, dtype=jnp.int32)[None, :] >= own_orders[:, None]).astype(F32)
    spectrum, above, below, mask = lax.optimization_barrier((spectrum, above, below, mask))
    spectrum = lax.all_to_all(
        spectrum.reshape(lat, -1, LANES), "lat", split_axis=0, concat_axis=0, tiled=True
    ).reshape(spectrum.shape)
    responses = disco_responses(above, field, below, support_blocks, filter_values)
    disco_sum = sum(
        jnp.dot(responses[tap].reshape(-1, channels), disco_weight[tap], preferred_element_type=F32)
        for tap in range(responses.shape[0])
    )
    spectrum, responses, disco_sum = lax.optimization_barrier((spectrum, responses, disco_sum))
    filtered = legendre_round_trip(legendre, mask[:, None, :], spectrum, pairs)
    filtered = lax.all_to_all(
        filtered.reshape(lat, -1, LANES), "lat", split_axis=0, concat_axis=0, tiled=True
    ).reshape(filtered.shape)
    west, east = turn(filtered, "lon", 1), turn(filtered, "lon", -1)
    middle = filtered.shape[0] // 2
    far_west, far_east = turn(west[:middle], "lon", 1), turn(east[middle:], "lon", -1)
    (own_grid,) = synthesize(synthesis_table, filtered)
    west_grid, east_grid = synthesize(synthesis_table, west, east)
    output, terms = finish(
        (own_grid, west_grid, east_grid, far_west, far_east),
        synthesis_table,
        responses,
        disco_sum,
        field,
        cotangent,
        spectral_weight.reshape(-1, channels),
    )
    sums = sum_everywhere(terms)
    spectral = spectral_weight.shape[0] * channels
    return (
        output,
        sums[:spectral].reshape(spectral_weight.shape),
        sums[spectral:].reshape(disco_weight.shape),
    )


def solution(mesh):
    placed = (
        P("lat", "lon", None),
        P("lat", "lon", None),
        P("lat", None, None),
        P("lat"),
        P(),
        P("lat", None),
        P(None, "lat", None, None),
        P(),
        P(),
    )
    return jax.shard_map(
        local,
        mesh=mesh,
        in_specs=placed,
        out_specs=(P("lat", "lon", None), P(), P()),
        check_vma=False,
    )
```

```python
import functools
import math

import jax
import jax.numpy as jnp
from jax import lax
from jax.experimental import pallas as pl
from jax.experimental.layout import Layout, with_layout_constraint
from jax.experimental.pallas import tpu as pltpu
from jax.sharding import PartitionSpec as P

F32 = jnp.float32
BF16 = jnp.bfloat16
LANES = 128
HALF = LANES // 2
GELU_SCALE = math.sqrt(2.0 / math.pi)
GELU_CUBE = 0.044715


def vmem_call(kernel, operands, out_shape, scratch=(), limit=32, far=()):
    place = pl.BlockSpec(memory_space=pltpu.VMEM)
    places = [pl.BlockSpec(memory_space=pl.ANY) if i in far else place for i in range(len(operands))]
    return pl.pallas_call(
        kernel,
        in_specs=places,
        out_specs=jax.tree.map(lambda _: place, out_shape),
        out_shape=out_shape,
        scratch_shapes=list(scratch),
        compiler_params=pltpu.CompilerParams(vmem_limit_bytes=limit << 20),
        cost_estimate=pl.CostEstimate(flops=0, bytes_accessed=1 << 20, transcendentals=0),
    )(*operands)


def low_lanes(rows):
    return lax.broadcasted_iota(jnp.int32, (rows, LANES), 1) < HALF


def swap(value):
    return pltpu.roll(value, HALF, 1)


def exchange(low, first, second):
    return (jnp.where(low, first, swap(second)), jnp.where(low, swap(first), second))


def pack_kernel(field_ref, *out_refs):
    rows, cols, _ = field_ref.shape
    parts = len(out_refs)
    low = low_lanes(cols)
    for ahead, out_ref in enumerate(out_refs):
        quarter = lax.rem(lax.axis_index("lon") + ahead, parts)
        upper = lax.rem(quarter, 2)
        lanes = pl.ds(pl.multiple_of((quarter // 2) * LANES, LANES), LANES)
        for pair in range(rows // 2):
            first = pltpu.roll(field_ref[2 * pair, :, lanes].astype(F32), upper * HALF, 1)
            second = pltpu.roll(field_ref[2 * pair + 1, :, lanes].astype(F32), HALF - upper * HALF, 1)
            out_ref[:, pair * LANES : (pair + 1) * LANES] = jnp.where(low, first, second).astype(BF16)


def pack(field):
    rows, cols, channels = field.shape
    parts = channels // HALF
    return vmem_call(
        pack_kernel, [field], [jax.ShapeDtypeStruct((cols, rows * HALF), BF16)] * parts
    )


def quarter_wave(units, nlon):
    angle = units * (2.0 * math.pi / nlon)
    square = angle * angle
    total = jnp.full_like(square, 1.0 / math.factorial(12))
    for power in (10, 8, 6, 4, 2, 0):
        total = total * square + (-1.0) ** (power // 2) / math.factorial(power)
    return total


def whole_mod_four(value):
    return value - 4.0 * jnp.floor(value * 0.25)


def wave(column, order, ahead, nlon):
    quarter = nlon // 4
    phase = column * order
    turns = jnp.floor((phase + 0.5) * (1.0 / quarter))
    rest = phase - turns * quarter
    cosine = quarter_wave(rest, nlon)
    sine = quarter_wave(quarter - rest, nlon)
    turns = whole_mod_four(turns + ahead)
    odd = (turns == 1.0) | (turns == 3.0)
    here = jnp.where(odd, sine, cosine)
    further = jnp.where(odd, cosine, sine)
    here = jnp.where((turns == 1.0) | (turns == 2.0), -here, here)
    further = jnp.where(turns < 1.5, -further, further)
    return (here, further)


def advance(here, further, turns):
    turns = whole_mod_four(turns)
    even = (turns == 0.0).astype(F32) - (turns == 2.0).astype(F32)
    odd = (turns == 1.0).astype(F32) - (turns == 3.0).astype(F32)
    return even * here + odd * further


def table_kernel(down_ref, across_ref, after_ref, analysis_ref, synthesis_ref):
    parts, rows, cols = analysis_ref.shape
    nlon = parts * cols
    place = lax.axis_index("lon")
    order, part = down_ref[:, 0:1], down_ref[:, 1:2]
    column = lax.broadcasted_iota(jnp.int32, (rows, cols), 1).astype(F32)
    here, further = wave(column, order, part, nlon)
    for k in range(parts):
        slab = lax.rem(place + parts - k, parts).astype(F32)
        analysis_ref[k] = advance(here, further, slab * order).astype(BF16)
    order, part = across_ref[0:1, :], across_ref[1:2, :]
    column = lax.broadcasted_iota(jnp.int32, (cols, rows), 0).astype(F32)
    here, further = wave(column, order, part, nlon)
    factor = jnp.where(order == 0.0, 1.0, 2.0)
    turns = place.astype(F32) * order
    for back in range(2):
        synthesis_ref[back] = (factor * advance(here, further, turns + back)).astype(BF16)


def fourier_tables(row_orders, row_parts, parts, after):
    coefs, cols = row_orders.shape[0], after.shape[0]
    both = jnp.stack([row_orders, row_parts]).astype(F32)
    return vmem_call(
        table_kernel,
        [both.T, both, after],
        [
            jax.ShapeDtypeStruct((parts, coefs, cols), BF16),
            jax.ShapeDtypeStruct((2, cols, coefs), BF16),
        ],
        far=(2,),
    )


def analysis_kernel(parts, table_ref, *refs):
    weight_ref, out_ref, wide_ref = refs[parts:]
    rows = table_ref.shape[1]
    total = jnp.dot(table_ref[0], refs[0][...], preferred_element_type=F32)
    for k in range(1, parts):
        total += jnp.dot(table_ref[k], refs[k][...], preferred_element_type=F32)
    total = total * weight_ref[...]
    pairs = total.shape[1] // LANES
    for pair in range(pairs):
        wide_ref[pl.ds(pair, rows, stride=pairs), :] = total[:, pair * LANES : (pair + 1) * LANES]
    out_ref[...] = wide_ref[...].astype(BF16)


def analysis(table, pieces, weight):
    parts, coefs, _ = table.shape
    shape = (coefs * weight.shape[1] // LANES, LANES)
    return vmem_call(
        functools.partial(analysis_kernel, parts),
        [table, *pieces, weight],
        jax.ShapeDtypeStruct(shape, BF16),
        [pltpu.VMEM(shape, F32)],
    )


def legendre_kernel(pairs, leg_ref, mask_ref, spec_ref, out_ref, wide_ref, lat_ref, back_ref):
    slots, nlat, _ = leg_ref.shape
    rows = 2 * pairs
    blocks = nlat // rows
    piece = 2 * slots * pairs
    low = low_lanes(blocks)
    wide_ref[...] = spec_ref[...].astype(F32)
    for slot in range(slots):
        lat = lat_ref.at[slot]

        def taken(part, pair):
            return pl.ds((part * slots + slot) * pairs + pair, blocks, stride=piece)

        for pair in range(pairs):
            even, odd = exchange(low, wide_ref[taken(0, pair), :], wide_ref[taken(1, pair), :])
            lat[pl.ds(2 * pair, blocks, stride=rows), :] = even
            lat[pl.ds(2 * pair + 1, blocks, stride=rows), :] = odd
        leg = leg_ref[slot]
        coeffs = lax.dot_general(
            lat[...].astype(BF16), leg, (((0,), (0,)), ((), ())), preferred_element_type=F32
        )
        coeffs = (coeffs * mask_ref[slot]).astype(BF16)
        lat[...] = lax.dot_general(leg, coeffs, (((1,), (1,)), ((), ())), preferred_element_type=F32)
        for pair in range(pairs):
            real, imag = exchange(
                low,
                lat[pl.ds(2 * pair, blocks, stride=rows), :],
                lat[pl.ds(2 * pair + 1, blocks, stride=rows), :],
            )
            back_ref[taken(0, pair), :] = real
            back_ref[taken(1, pair), :] = imag
    out_ref[...] = back_ref[...].astype(BF16)


def legendre_round_trip(legendre, mask, spectrum, pairs):
    slots, nlat, _ = legendre.shape
    return vmem_call(
        functools.partial(legendre_kernel, pairs),
        [legendre, mask, spectrum],
        jax.ShapeDtypeStruct(spectrum.shape, BF16),
        [
            pltpu.VMEM(spectrum.shape, F32),
            pltpu.VMEM((slots, nlat, LANES), F32),
            pltpu.VMEM(spectrum.shape, F32),
        ],
    )


def synthesis(table_ref, wide_ref, pairs):
    coefs = table_ref.shape[2]
    held = [wide_ref[pl.ds(pair, coefs, stride=pairs), :] for pair in range(pairs)]
    spectrum = jnp.concatenate(held, axis=1).astype(BF16)
    return [
        jnp.dot(table_ref[part], spectrum, preferred_element_type=F32)
        for part in range(table_ref.shape[0])
    ]


def synthesis_kernel(table_ref, *refs):
    wide_ref = refs[-1]
    count = len(refs) // 2
    for in_ref, out_ref in zip(refs[:count], refs[count:-1]):
        wide_ref[...] = in_ref[...].astype(F32)
        pairs = out_ref.shape[1]
        for part, grid in enumerate(synthesis(table_ref, wide_ref, pairs)):
            for pair in range(pairs):
                out_ref[part, pair] = grid[:, pair * LANES : (pair + 1) * LANES].astype(BF16)


def synthesize(table, *spectra):
    parts, cols, coefs = table.shape
    rows = spectra[0].shape[0]
    shape = jax.ShapeDtypeStruct((parts, rows // coefs, cols, LANES), BF16)
    return vmem_call(
        synthesis_kernel,
        [table, *spectra],
        [shape] * len(spectra),
        [pltpu.VMEM((rows, LANES), F32)],
    )


def finish_kernel(
    own_ref,
    west_ref,
    east_ref,
    far_west_ref,
    far_east_ref,
    table_ref,
    resp_ref,
    disco_ref,
    field_ref,
    cot_ref,
    weight_ref,
    out_ref,
    grad_ref,
    wide_ref,
    mix_ref,
    total_ref,
):
    pairs, _, channels = field_ref.shape
    cols = table_ref.shape[1]
    middle = far_west_ref.shape[0]
    low = low_lanes(cols)
    place = lax.axis_index("lon")
    odd = lax.rem(place, 2) == 1
    near = place // 2
    wide_ref[:middle] = far_west_ref[...].astype(F32)
    wide_ref[middle:] = far_east_ref[...].astype(F32)
    far_grid = synthesis(table_ref, wide_ref, pairs)
    for pair in range(pairs):
        mix = mix_ref.at[pair]
        for part in range(2):
            own, west, east = (
                ref[part, pair].astype(F32) for ref in (own_ref, west_ref, east_ref)
            )
            far = far_grid[part][:, pair * LANES : (pair + 1) * LANES]
            tiles = [
                (near, jnp.where(odd, west, own), jnp.where(odd, own, east)),
                (1 - near, jnp.where(odd, east, far), jnp.where(odd, far, west)),
            ]
            for tile, first, second in tiles:
                start = pl.multiple_of(part * channels + tile * LANES, LANES)
                grid = jnp.concatenate(exchange(low, first, second), axis=0).astype(BF16)
                mix[:, pl.ds(start, LANES)] = grid
        pre = jnp.dot(mix[...], weight_ref[...], preferred_element_type=F32) + disco_ref[pair]
        square = pre * pre
        bend = jnp.tanh(GELU_SCALE * (pre + GELU_CUBE * (square * pre)))
        activated = 0.5 * pre * (1.0 + bend)
        slope = 0.5 * (1.0 + bend) + 0.5 * pre * (1.0 - bend * bend) * (
            GELU_SCALE * (1.0 + 3.0 * GELU_CUBE * square)
        )
        out_ref[pair] = (field_ref[pair].astype(F32) + activated).astype(BF16)
        grad_pre = (cot_ref[pair].astype(F32) * slope).astype(BF16)
        start = 0
        for values in [mix[...]] + [resp_ref[tap, pair] for tap in range(resp_ref.shape[0])]:
            term = lax.dot_general(
                grad_pre, values, (((0,), (0,)), ((), ())), preferred_element_type=F32
            )
            span = slice(start, start + values.shape[1])
            start = span.stop
            if pair == 0:
                total_ref[:, span] = term
            else:
                total_ref[:, span] += term
    for part in range(grad_ref.shape[0] // channels):
        span = slice(part * channels, (part + 1) * channels)
        grad_ref[span, :] = total_ref[:, span].T.astype(BF16)


def finish(spectra, table, responses, disco_sum, field, cotangent, weight):
    rows, cols, channels = field.shape
    pairs = rows // 2
    grouped = (pairs, 2 * cols, channels)
    taps = responses.shape[0]
    stacked = weight.shape[0] + taps * channels
    output, grads = vmem_call(
        finish_kernel,
        [
            *spectra,
            table,
            responses.reshape(taps, *grouped),
            disco_sum.reshape(grouped),
            field.reshape(grouped),
            cotangent.reshape(grouped),
            weight,
        ],
        [jax.ShapeDtypeStruct(grouped, BF16), jax.ShapeDtypeStruct((stacked, channels), BF16)],
        [
            pltpu.VMEM((pairs * table.shape[2], LANES), F32),
            pltpu.VMEM((pairs, 2 * cols, weight.shape[0]), BF16),
            pltpu.VMEM((channels, stacked), F32),
        ],
    )
    return output.reshape(field.shape), grads


def turn(value, axis, by):
    size = lax.axis_size(axis)
    return lax.ppermute(value, axis, [(i, (i + by) % size) for i in range(size)])


def disco_responses(above, field, below, support_blocks, filter_values):
    rows, cols, _ = field.shape
    lat_pos = lax.axis_index("lat")
    blocks = jnp.concatenate([above, field, below], axis=0)
    picks = support_blocks[0] - lat_pos + 1
    onehot = (picks[:, None] == jnp.arange(3, dtype=jnp.int32)[None, :]).astype(F32)
    operator = (
        jnp.einsum("tasb,sq->taqb", filter_values.astype(F32), onehot)
        .reshape(3, rows, 3 * rows)
        .astype(BF16)
    )
    here, level, there = (
        jnp.einsum("ab,boc->aoc", operator[tap], blocks, preferred_element_type=F32).astype(BF16)
        for tap in range(3)
    )
    first = turn(here[:, cols - 1 :], "lon", 1)
    last = turn(there[:, :1], "lon", -1)
    return jnp.stack(
        [
            jnp.concatenate([first, here[:, : cols - 1]], axis=1),
            level,
            jnp.concatenate([there[:, 1:], last], axis=1),
        ]
    )


def sum_everywhere(terms):
    rows, channels = terms.shape
    lon, lat = lax.axis_size("lon"), lax.axis_size("lat")
    side = 8 if lat % 8 == 0 else lat
    count = side * lon
    planes = [list(range(z * count, (z + 1) * count)) for z in range(lat // side)]
    columns = [list(range(i, lat, side)) for i in range(side)]
    share = rows // count
    pieces = lax.all_to_all(
        terms.reshape(count, share, channels),
        ("lat", "lon"),
        0,
        0,
        tiled=True,
        axis_index_groups=planes,
    )
    own = jnp.sum(pieces.astype(F32), axis=0).astype(BF16)
    others = lax.all_to_all(
        jnp.broadcast_to(own[None], (lat // side, share, channels)),
        "lat",
        0,
        0,
        tiled=True,
        axis_index_groups=columns,
    )
    total = jnp.sum(others.astype(F32), axis=0).astype(BF16)
    everything = lax.all_to_all(
        jnp.broadcast_to(total[None], (count, share, channels)),
        ("lat", "lon"),
        0,
        0,
        tiled=True,
        axis_index_groups=planes,
    )
    return everything.reshape(rows, channels)


def local(
    field,
    cotangent,
    legendre,
    quad_weight,
    order_slots,
    support_blocks,
    filter_values,
    spectral_weight,
    disco_weight,
):
    rows, cols, channels = field.shape
    lat, lon = lax.axis_size("lat"), lax.axis_size("lon")
    nlon = cols * lon
    slots, nlat, degrees = legendre.shape
    pairs = rows // 2
    lat_pos, lon_pos = lax.axis_index("lat"), lax.axis_index("lon")

    pieces = pack(field)
    slabs = [pieces[0]] + [turn(pieces[k], "lon", k) for k in range(1, lon)]

    row_orders = jnp.broadcast_to(order_slots.reshape(lat, 1, slots), (lat, 2, slots)).reshape(-1)
    row_parts = jnp.broadcast_to(
        jnp.arange(2, dtype=jnp.int32)[None, :, None], (lat, 2, slots)
    ).reshape(-1)
    above, below = (
        with_layout_constraint(turn(field, "lat", way), Layout((0, 1, 2))) for way in (1, -1)
    )
    analysis_table, synthesis_table = fourier_tables(row_orders, row_parts, lon, pieces[0])
    lane_weight = jnp.repeat(quad_weight * (1.0 / nlon), HALF)[None, :]
    spectrum = analysis(analysis_table, slabs, lane_weight)
    own_orders = lax.dynamic_slice_in_dim(order_slots, lat_pos * slots, slots)
    mask = (jnp.arange(degrees, dtype=jnp.int32)[None, :] >= own_orders[:, None]).astype(F32)
    spectrum, mask = lax.optimization_barrier((spectrum, mask))
    spectrum = lax.all_to_all(
        spectrum.reshape(lat, -1, LANES), "lat", split_axis=0, concat_axis=0, tiled=True
    ).reshape(spectrum.shape)
    responses = disco_responses(above, field, below, support_blocks, filter_values)
    disco_sum = sum(
        jnp.dot(responses[tap].reshape(-1, channels), disco_weight[tap], preferred_element_type=F32)
        for tap in range(responses.shape[0])
    )
    spectrum, responses, disco_sum = lax.optimization_barrier((spectrum, responses, disco_sum))
    filtered = legendre_round_trip(legendre, mask[:, None, :], spectrum, pairs)
    filtered = lax.all_to_all(
        filtered.reshape(lat, -1, LANES), "lat", split_axis=0, concat_axis=0, tiled=True
    ).reshape(filtered.shape)
    west, east = turn(filtered, "lon", 1), turn(filtered, "lon", -1)
    middle = filtered.shape[0] // 2
    far_west, far_east = turn(west[:middle], "lon", 1), turn(east[middle:], "lon", -1)
    (own_grid,) = synthesize(synthesis_table, filtered)
    west_grid, east_grid = synthesize(synthesis_table, west, east)
    output, terms = finish(
        (own_grid, west_grid, east_grid, far_west, far_east),
        synthesis_table,
        responses,
        disco_sum,
        field,
        cotangent,
        spectral_weight.reshape(-1, channels),
    )
    sums = sum_everywhere(terms)
    spectral = spectral_weight.shape[0] * channels
    return (
        output,
        sums[:spectral].reshape(spectral_weight.shape).astype(F32),
        sums[spectral:].reshape(disco_weight.shape).astype(F32),
    )


def solution(mesh):
    placed = (
        P("lat", "lon", None),
        P("lat", "lon", None),
        P("lat", None, None),
        P("lat"),
        P(),
        P("lat", None),
        P(None, "lat", None, None),
        P(),
        P(),
    )
    return jax.shard_map(
        local,
        mesh=mesh,
        in_specs=placed,
        out_specs=(P("lat", "lon", None), P(), P()),
        check_vma=False,
    )
```

```python
import functools
import math

import jax
import jax.numpy as jnp
from jax import lax
from jax.experimental import pallas as pl
from jax.experimental.layout import Layout, with_layout_constraint
from jax.experimental.pallas import tpu as pltpu
from jax.sharding import PartitionSpec as P

F32 = jnp.float32
BF16 = jnp.bfloat16
LANES = 128
HALF = LANES // 2
GELU_SCALE = math.sqrt(2.0 / math.pi)
GELU_CUBE = 0.044715


def vmem_call(kernel, operands, out_shape, scratch=(), limit=32, far=()):
    place = pl.BlockSpec(memory_space=pltpu.VMEM)
    places = [pl.BlockSpec(memory_space=pl.ANY) if i in far else place for i in range(len(operands))]
    return pl.pallas_call(
        kernel,
        in_specs=places,
        out_specs=jax.tree.map(lambda _: place, out_shape),
        out_shape=out_shape,
        scratch_shapes=list(scratch),
        compiler_params=pltpu.CompilerParams(vmem_limit_bytes=limit << 20),
        cost_estimate=pl.CostEstimate(flops=0, bytes_accessed=1 << 20, transcendentals=0),
    )(*operands)


def low_lanes(rows):
    return lax.broadcasted_iota(jnp.int32, (rows, LANES), 1) < HALF


def swap(value):
    return pltpu.roll(value, HALF, 1)


def exchange(low, first, second):
    return (jnp.where(low, first, swap(second)), jnp.where(low, swap(first), second))


def pack_kernel(field_ref, *out_refs):
    rows, cols, _ = field_ref.shape
    parts = len(out_refs)
    low = low_lanes(cols)
    for ahead, out_ref in enumerate(out_refs):
        quarter = lax.rem(lax.axis_index("lon") + ahead, parts)
        upper = lax.rem(quarter, 2)
        lanes = pl.ds(pl.multiple_of((quarter // 2) * LANES, LANES), LANES)
        for pair in range(rows // 2):
            first = pltpu.roll(field_ref[2 * pair, :, lanes].astype(F32), upper * HALF, 1)
            second = pltpu.roll(field_ref[2 * pair + 1, :, lanes].astype(F32), HALF - upper * HALF, 1)
            out_ref[:, pair * LANES : (pair + 1) * LANES] = jnp.where(low, first, second).astype(BF16)


def pack(field):
    rows, cols, channels = field.shape
    parts = channels // HALF
    return vmem_call(
        pack_kernel, [field], [jax.ShapeDtypeStruct((cols, rows * HALF), BF16)] * parts
    )


def quarter_wave(units, nlon):
    angle = units * (2.0 * math.pi / nlon)
    square = angle * angle
    total = jnp.full_like(square, 1.0 / math.factorial(12))
    for power in (10, 8, 6, 4, 2, 0):
        total = total * square + (-1.0) ** (power // 2) / math.factorial(power)
    return total


def whole_mod_four(value):
    return value - 4.0 * jnp.floor(value * 0.25)


def wave(column, order, ahead, nlon):
    quarter = nlon // 4
    phase = column * order
    turns = jnp.floor((phase + 0.5) * (1.0 / quarter))
    rest = phase - turns * quarter
    cosine = quarter_wave(rest, nlon)
    sine = quarter_wave(quarter - rest, nlon)
    turns = whole_mod_four(turns + ahead)
    odd = (turns == 1.0) | (turns == 3.0)
    here = jnp.where(odd, sine, cosine)
    further = jnp.where(odd, cosine, sine)
    here = jnp.where((turns == 1.0) | (turns == 2.0), -here, here)
    further = jnp.where(turns < 1.5, -further, further)
    return (here, further)


def advance(here, further, turns):
    turns = whole_mod_four(turns)
    even = (turns == 0.0).astype(F32) - (turns == 2.0).astype(F32)
    odd = (turns == 1.0).astype(F32) - (turns == 3.0).astype(F32)
    return even * here + odd * further


def table_kernel(down_ref, across_ref, after_ref, analysis_ref, synthesis_ref):
    parts, rows, cols = analysis_ref.shape
    nlon = parts * cols
    place = lax.axis_index("lon")
    order, part = down_ref[:, 0:1], down_ref[:, 1:2]
    column = lax.broadcasted_iota(jnp.int32, (rows, cols), 1).astype(F32)
    here, further = wave(column, order, part, nlon)
    for k in range(parts):
        slab = lax.rem(place + parts - k, parts).astype(F32)
        analysis_ref[k] = advance(here, further, slab * order).astype(BF16)
    order, part = across_ref[0:1, :], across_ref[1:2, :]
    column = lax.broadcasted_iota(jnp.int32, (cols, rows), 0).astype(F32)
    here, further = wave(column, order, part, nlon)
    factor = jnp.where(order == 0.0, 1.0, 2.0)
    turns = place.astype(F32) * order
    for back in range(2):
        synthesis_ref[back] = (factor * advance(here, further, turns + back)).astype(BF16)


def fourier_tables(row_orders, row_parts, parts, after):
    coefs, cols = row_orders.shape[0], after.shape[0]
    both = jnp.stack([row_orders, row_parts]).astype(F32)
    return vmem_call(
        table_kernel,
        [both.T, both, after],
        [
            jax.ShapeDtypeStruct((parts, coefs, cols), BF16),
            jax.ShapeDtypeStruct((2, cols, coefs), BF16),
        ],
        far=(2,),
    )


def analysis_kernel(parts, table_ref, *refs):
    weight_ref, out_ref, wide_ref = refs[parts:]
    rows = table_ref.shape[1]
    total = jnp.dot(table_ref[0], refs[0][...], preferred_element_type=F32)
    for k in range(1, parts):
        total += jnp.dot(table_ref[k], refs[k][...], preferred_element_type=F32)
    total = total * weight_ref[...]
    pairs = total.shape[1] // LANES
    for pair in range(pairs):
        wide_ref[pl.ds(pair, rows, stride=pairs), :] = total[:, pair * LANES : (pair + 1) * LANES]
    out_ref[...] = wide_ref[...].astype(BF16)


def analysis(table, pieces, weight):
    parts, coefs, _ = table.shape
    shape = (coefs * weight.shape[1] // LANES, LANES)
    return vmem_call(
        functools.partial(analysis_kernel, parts),
        [table, *pieces, weight],
        jax.ShapeDtypeStruct(shape, BF16),
        [pltpu.VMEM(shape, F32)],
    )


def legendre_kernel(pairs, leg_ref, mask_ref, spec_ref, out_ref, wide_ref, lat_ref, back_ref):
    slots, nlat, _ = leg_ref.shape
    rows = 2 * pairs
    blocks = nlat // rows
    piece = 2 * slots * pairs
    low = low_lanes(blocks)
    wide_ref[...] = spec_ref[...].astype(F32)
    for slot in range(slots):
        lat = lat_ref.at[slot]

        def taken(part, pair):
            return pl.ds((part * slots + slot) * pairs + pair, blocks, stride=piece)

        for pair in range(pairs):
            even, odd = exchange(low, wide_ref[taken(0, pair), :], wide_ref[taken(1, pair), :])
            lat[pl.ds(2 * pair, blocks, stride=rows), :] = even
            lat[pl.ds(2 * pair + 1, blocks, stride=rows), :] = odd
        leg = leg_ref[slot]
        coeffs = lax.dot_general(
            lat[...].astype(BF16), leg, (((0,), (0,)), ((), ())), preferred_element_type=F32
        )
        coeffs = (coeffs * mask_ref[slot]).astype(BF16)
        lat[...] = lax.dot_general(leg, coeffs, (((1,), (1,)), ((), ())), preferred_element_type=F32)
        for pair in range(pairs):
            real, imag = exchange(
                low,
                lat[pl.ds(2 * pair, blocks, stride=rows), :],
                lat[pl.ds(2 * pair + 1, blocks, stride=rows), :],
            )
            back_ref[taken(0, pair), :] = real
            back_ref[taken(1, pair), :] = imag
    out_ref[...] = back_ref[...].astype(BF16)


def legendre_round_trip(legendre, mask, spectrum, pairs):
    slots, nlat, _ = legendre.shape
    return vmem_call(
        functools.partial(legendre_kernel, pairs),
        [legendre, mask, spectrum],
        jax.ShapeDtypeStruct(spectrum.shape, BF16),
        [
            pltpu.VMEM(spectrum.shape, F32),
            pltpu.VMEM((slots, nlat, LANES), F32),
            pltpu.VMEM(spectrum.shape, F32),
        ],
    )


def synthesis(table_ref, wide_ref, pairs):
    coefs = table_ref.shape[2]
    held = [wide_ref[pl.ds(pair, coefs, stride=pairs), :] for pair in range(pairs)]
    spectrum = jnp.concatenate(held, axis=1).astype(BF16)
    return [
        jnp.dot(table_ref[part], spectrum, preferred_element_type=F32)
        for part in range(table_ref.shape[0])
    ]


def synthesis_kernel(table_ref, *refs):
    wide_ref = refs[-1]
    count = len(refs) // 2
    for in_ref, out_ref in zip(refs[:count], refs[count:-1]):
        wide_ref[...] = in_ref[...].astype(F32)
        pairs = out_ref.shape[1]
        for part, grid in enumerate(synthesis(table_ref, wide_ref, pairs)):
            for pair in range(pairs):
                out_ref[part, pair] = grid[:, pair * LANES : (pair + 1) * LANES].astype(BF16)


def synthesize(table, *spectra):
    parts, cols, coefs = table.shape
    rows = spectra[0].shape[0]
    shape = jax.ShapeDtypeStruct((parts, rows // coefs, cols, LANES), BF16)
    return vmem_call(
        synthesis_kernel,
        [table, *spectra],
        [shape] * len(spectra),
        [pltpu.VMEM((rows, LANES), F32)],
    )


def finish_kernel(
    own_ref,
    west_ref,
    east_ref,
    far_west_ref,
    far_east_ref,
    table_ref,
    resp_ref,
    disco_ref,
    field_ref,
    cot_ref,
    weight_ref,
    out_ref,
    kept_ref,
    given_ref,
    wide_ref,
    mix_ref,
    total_ref,
):
    pairs, _, channels = field_ref.shape
    cols = table_ref.shape[1]
    middle = far_west_ref.shape[0]
    low = low_lanes(cols)
    place = lax.axis_index("lon")
    odd = lax.rem(place, 2) == 1
    near = place // 2
    wide_ref[:middle] = far_west_ref[...].astype(F32)
    wide_ref[middle:] = far_east_ref[...].astype(F32)
    far_grid = synthesis(table_ref, wide_ref, pairs)
    for pair in range(pairs):
        mix = mix_ref.at[pair]
        for part in range(2):
            own, west, east = (
                ref[part, pair].astype(F32) for ref in (own_ref, west_ref, east_ref)
            )
            far = far_grid[part][:, pair * LANES : (pair + 1) * LANES]
            tiles = [
                (near, jnp.where(odd, west, own), jnp.where(odd, own, east)),
                (1 - near, jnp.where(odd, east, far), jnp.where(odd, far, west)),
            ]
            for tile, first, second in tiles:
                start = pl.multiple_of(part * channels + tile * LANES, LANES)
                grid = jnp.concatenate(exchange(low, first, second), axis=0).astype(BF16)
                mix[:, pl.ds(start, LANES)] = grid
        pre = jnp.dot(mix[...], weight_ref[...], preferred_element_type=F32) + disco_ref[pair]
        square = pre * pre
        bend = jnp.tanh(GELU_SCALE * (pre + GELU_CUBE * (square * pre)))
        activated = 0.5 * pre * (1.0 + bend)
        slope = 0.5 * (1.0 + bend) + 0.5 * pre * (1.0 - bend * bend) * (
            GELU_SCALE * (1.0 + 3.0 * GELU_CUBE * square)
        )
        out_ref[pair] = (field_ref[pair].astype(F32) + activated).astype(BF16)
        grad_pre = (cot_ref[pair].astype(F32) * slope).astype(BF16)
        start = 0
        for values in [mix[...]] + [resp_ref[tap, pair] for tap in range(resp_ref.shape[0])]:
            term = lax.dot_general(
                grad_pre, values, (((0,), (0,)), ((), ())), preferred_element_type=F32
            )
            span = slice(start, start + values.shape[1])
            start = span.stop
            if pair == 0:
                total_ref[:, span] = term
            else:
                total_ref[:, span] += term
    first = lax.rem(lax.axis_index("lat"), 2) == 0
    half = kept_ref.shape[0]
    for start in range(0, half, LANES):
        span = slice(start, start + LANES)
        early = total_ref[:, span].T
        late = total_ref[:, half + start : half + start + LANES].T
        kept_ref[span, :] = jnp.where(first, early, late).astype(BF16)
        given_ref[span, :] = jnp.where(first, late, early).astype(BF16)


def finish(spectra, table, responses, disco_sum, field, cotangent, weight):
    rows, cols, channels = field.shape
    pairs = rows // 2
    grouped = (pairs, 2 * cols, channels)
    taps = responses.shape[0]
    stacked = weight.shape[0] + taps * channels
    half = jax.ShapeDtypeStruct((stacked // 2, channels), BF16)
    output, kept, given = vmem_call(
        finish_kernel,
        [
            *spectra,
            table,
            responses.reshape(taps, *grouped),
            disco_sum.reshape(grouped),
            field.reshape(grouped),
            cotangent.reshape(grouped),
            weight,
        ],
        [jax.ShapeDtypeStruct(grouped, BF16), half, half],
        [
            pltpu.VMEM((pairs * table.shape[2], LANES), F32),
            pltpu.VMEM((pairs, 2 * cols, weight.shape[0]), BF16),
            pltpu.VMEM((channels, stacked), F32),
        ],
    )
    return output.reshape(field.shape), kept, given


def turn(value, axis, by):
    size = lax.axis_size(axis)
    return lax.ppermute(value, axis, [(i, (i + by) % size) for i in range(size)])


def disco_responses(above, field, below, support_blocks, filter_values):
    rows, cols, _ = field.shape
    lat_pos = lax.axis_index("lat")
    blocks = jnp.concatenate([above, field, below], axis=0)
    picks = support_blocks[0] - lat_pos + 1
    onehot = (picks[:, None] == jnp.arange(3, dtype=jnp.int32)[None, :]).astype(F32)
    operator = (
        jnp.einsum("tasb,sq->taqb", filter_values.astype(F32), onehot)
        .reshape(3, rows, 3 * rows)
        .astype(BF16)
    )
    here, level, there = (
        jnp.einsum("ab,boc->aoc", operator[tap], blocks, preferred_element_type=F32).astype(BF16)
        for tap in range(3)
    )
    first = turn(here[:, cols - 1 :], "lon", 1)
    last = turn(there[:, :1], "lon", -1)
    return jnp.stack(
        [
            jnp.concatenate([first, here[:, : cols - 1]], axis=1),
            level,
            jnp.concatenate([there[:, 1:], last], axis=1),
        ]
    )


def shares(value, axis, groups):
    return lax.all_to_all(value, axis, 0, 0, tiled=True, axis_index_groups=groups)


def sum_everywhere(kept, given):
    half, channels = kept.shape
    lon, lat = lax.axis_size("lon"), lax.axis_size("lat")
    side = 8 if lat % 8 == 0 else lat
    planes = [
        [(z * side + i) * lon + x for i in range(core, side, 2) for x in range(lon)]
        for z in range(lat // side)
        for core in range(2)
    ]
    columns = [list(range(i, lat, side)) for i in range(side)]
    count, depth = len(planes[0]), len(columns[0])

    def swap_cores(value):
        return lax.ppermute(value, "lat", [(i, i ^ 1) for i in range(lat)])

    def total(pieces):
        return jnp.sum(pieces.astype(F32), axis=0).astype(BF16)

    def copies(value, number):
        return jnp.broadcast_to(value[None], (number, *value.shape))

    core = lax.rem(lax.axis_index("lat"), 2)
    both = (kept.astype(F32) + swap_cores(given).astype(F32)).astype(BF16)
    share = half // count
    own = total(shares(both.reshape(count, share, channels), ("lat", "lon"), planes))
    own = total(shares(copies(own, depth), "lat", columns))
    mine = shares(copies(own, count), ("lat", "lon"), planes).reshape(half, channels)
    other = swap_cores(mine)
    first = jnp.where(core == 0, mine, other)
    second = jnp.where(core == 0, other, mine)
    return jnp.concatenate([first, second])


def local(
    field,
    cotangent,
    legendre,
    quad_weight,
    order_slots,
    support_blocks,
    filter_values,
    spectral_weight,
    disco_weight,
):
    rows, cols, channels = field.shape
    lat, lon = lax.axis_size("lat"), lax.axis_size("lon")
    nlon = cols * lon
    slots, nlat, degrees = legendre.shape
    pairs = rows // 2
    lat_pos, lon_pos = lax.axis_index("lat"), lax.axis_index("lon")

    pieces = pack(field)
    slabs = [pieces[0]] + [turn(pieces[k], "lon", k) for k in range(1, lon)]

    row_orders = jnp.broadcast_to(order_slots.reshape(lat, 1, slots), (lat, 2, slots)).reshape(-1)
    row_parts = jnp.broadcast_to(
        jnp.arange(2, dtype=jnp.int32)[None, :, None], (lat, 2, slots)
    ).reshape(-1)
    above, below = (
        with_layout_constraint(turn(field, "lat", way), Layout((0, 1, 2))) for way in (1, -1)
    )
    analysis_table, synthesis_table = fourier_tables(row_orders, row_parts, lon, pieces[0])
    lane_weight = jnp.repeat(quad_weight * (1.0 / nlon), HALF)[None, :]
    spectrum = analysis(analysis_table, slabs, lane_weight)
    own_orders = lax.dynamic_slice_in_dim(order_slots, lat_pos * slots, slots)
    mask = (jnp.arange(degrees, dtype=jnp.int32)[None, :] >= own_orders[:, None]).astype(F32)
    spectrum, mask = lax.optimization_barrier((spectrum, mask))
    spectrum = lax.all_to_all(
        spectrum.reshape(lat, -1, LANES), "lat", split_axis=0, concat_axis=0, tiled=True
    ).reshape(spectrum.shape)
    responses = disco_responses(above, field, below, support_blocks, filter_values)
    disco_sum = sum(
        jnp.dot(responses[tap].reshape(-1, channels), disco_weight[tap], preferred_element_type=F32)
        for tap in range(responses.shape[0])
    )
    spectrum, responses, disco_sum = lax.optimization_barrier((spectrum, responses, disco_sum))
    filtered = legendre_round_trip(legendre, mask[:, None, :], spectrum, pairs)
    filtered = lax.all_to_all(
        filtered.reshape(lat, -1, LANES), "lat", split_axis=0, concat_axis=0, tiled=True
    ).reshape(filtered.shape)
    west, east = turn(filtered, "lon", 1), turn(filtered, "lon", -1)
    middle = filtered.shape[0] // 2
    far_west, far_east = turn(west[:middle], "lon", 1), turn(east[middle:], "lon", -1)
    (own_grid,) = synthesize(synthesis_table, filtered)
    west_grid, east_grid = synthesize(synthesis_table, west, east)
    output, kept, given = finish(
        (own_grid, west_grid, east_grid, far_west, far_east),
        synthesis_table,
        responses,
        disco_sum,
        field,
        cotangent,
        spectral_weight.reshape(-1, channels),
    )
    sums = sum_everywhere(kept, given)
    spectral = spectral_weight.shape[0] * channels
    return (
        output,
        sums[:spectral].reshape(spectral_weight.shape).astype(F32),
        sums[spectral:].reshape(disco_weight.shape).astype(F32),
    )


def solution(mesh):
    placed = (
        P("lat", "lon", None),
        P("lat", "lon", None),
        P("lat", None, None),
        P("lat"),
        P(),
        P("lat", None),
        P(None, "lat", None, None),
        P(),
        P(),
    )
    return jax.shard_map(
        local,
        mesh=mesh,
        in_specs=placed,
        out_specs=(P("lat", "lon", None), P(), P()),
        check_vma=False,
    )
```

```python
import functools
import math

import jax
import jax.numpy as jnp
from jax import lax
from jax.experimental import pallas as pl
from jax.experimental.layout import Layout, with_layout_constraint
from jax.experimental.pallas import tpu as pltpu
from jax.sharding import PartitionSpec as P

F32 = jnp.float32
BF16 = jnp.bfloat16
LANES = 128
HALF = LANES // 2
GELU_SCALE = math.sqrt(2.0 / math.pi)
GELU_CUBE = 0.044715


def vmem_call(kernel, operands, out_shape, scratch=(), limit=32, far=()):
    place = pl.BlockSpec(memory_space=pltpu.VMEM)
    places = [pl.BlockSpec(memory_space=pl.ANY) if i in far else place for i in range(len(operands))]
    return pl.pallas_call(
        kernel,
        in_specs=places,
        out_specs=jax.tree.map(lambda _: place, out_shape),
        out_shape=out_shape,
        scratch_shapes=list(scratch),
        compiler_params=pltpu.CompilerParams(vmem_limit_bytes=limit << 20),
        cost_estimate=pl.CostEstimate(flops=0, bytes_accessed=1 << 20, transcendentals=0),
    )(*operands)


def low_lanes(rows):
    return lax.broadcasted_iota(jnp.int32, (rows, LANES), 1) < HALF


def swap(value):
    return pltpu.roll(value, HALF, 1)


def exchange(low, first, second):
    return (jnp.where(low, first, swap(second)), jnp.where(low, swap(first), second))


def pack_kernel(field_ref, *out_refs):
    rows, cols, _ = field_ref.shape
    parts = len(out_refs)
    low = low_lanes(cols)
    for ahead, out_ref in enumerate(out_refs):
        quarter = lax.rem(lax.axis_index("lon") + ahead, parts)
        upper = lax.rem(quarter, 2)
        lanes = pl.ds(pl.multiple_of((quarter // 2) * LANES, LANES), LANES)
        for pair in range(rows // 2):
            first = pltpu.roll(field_ref[2 * pair, :, lanes].astype(F32), upper * HALF, 1)
            second = pltpu.roll(field_ref[2 * pair + 1, :, lanes].astype(F32), HALF - upper * HALF, 1)
            out_ref[:, pair * LANES : (pair + 1) * LANES] = jnp.where(low, first, second).astype(BF16)


def pack(field):
    rows, cols, channels = field.shape
    parts = channels // HALF
    return vmem_call(
        pack_kernel, [field], [jax.ShapeDtypeStruct((cols, rows * HALF), BF16)] * parts
    )


def quarter_wave(units, nlon):
    angle = units * (2.0 * math.pi / nlon)
    square = angle * angle
    total = jnp.full_like(square, 1.0 / math.factorial(12))
    for power in (10, 8, 6, 4, 2, 0):
        total = total * square + (-1.0) ** (power // 2) / math.factorial(power)
    return total


def whole_mod_four(value):
    return value - 4.0 * jnp.floor(value * 0.25)


def wave(column, order, ahead, nlon):
    quarter = nlon // 4
    phase = column * order
    turns = jnp.floor((phase + 0.5) * (1.0 / quarter))
    rest = phase - turns * quarter
    cosine = quarter_wave(rest, nlon)
    sine = quarter_wave(quarter - rest, nlon)
    turns = whole_mod_four(turns + ahead)
    odd = (turns == 1.0) | (turns == 3.0)
    here = jnp.where(odd, sine, cosine)
    further = jnp.where(odd, cosine, sine)
    here = jnp.where((turns == 1.0) | (turns == 2.0), -here, here)
    further = jnp.where(turns < 1.5, -further, further)
    return (here, further)


def advance(here, further, turns):
    turns = whole_mod_four(turns)
    even = (turns == 0.0).astype(F32) - (turns == 2.0).astype(F32)
    odd = (turns == 1.0).astype(F32) - (turns == 3.0).astype(F32)
    return even * here + odd * further


def table_kernel(down_ref, across_ref, after_ref, analysis_ref, synthesis_ref):
    parts, rows, cols = analysis_ref.shape
    nlon = parts * cols
    place = lax.axis_index("lon")
    order, part = down_ref[:, 0:1], down_ref[:, 1:2]
    column = lax.broadcasted_iota(jnp.int32, (rows, cols), 1).astype(F32)
    here, further = wave(column, order, part, nlon)
    for k in range(parts):
        slab = lax.rem(place + parts - k, parts).astype(F32)
        analysis_ref[k] = advance(here, further, slab * order).astype(BF16)
    order, part = across_ref[0:1, :], across_ref[1:2, :]
    column = lax.broadcasted_iota(jnp.int32, (cols, rows), 0).astype(F32)
    here, further = wave(column, order, part, nlon)
    factor = jnp.where(order == 0.0, 1.0, 2.0)
    turns = place.astype(F32) * order
    for back in range(2):
        synthesis_ref[back] = (factor * advance(here, further, turns + back)).astype(BF16)


def fourier_tables(row_orders, row_parts, parts, after):
    coefs, cols = row_orders.shape[0], after.shape[0]
    both = jnp.stack([row_orders, row_parts]).astype(F32)
    return vmem_call(
        table_kernel,
        [both.T, both, after],
        [
            jax.ShapeDtypeStruct((parts, coefs, cols), BF16),
            jax.ShapeDtypeStruct((2, cols, coefs), BF16),
        ],
        far=(2,),
    )


def analysis_kernel(parts, table_ref, *refs):
    weight_ref, out_ref, wide_ref = refs[parts:]
    rows = table_ref.shape[1]
    total = jnp.dot(table_ref[0], refs[0][...], preferred_element_type=F32)
    for k in range(1, parts):
        total += jnp.dot(table_ref[k], refs[k][...], preferred_element_type=F32)
    total = total * weight_ref[...]
    pairs = total.shape[1] // LANES
    for pair in range(pairs):
        wide_ref[pl.ds(pair, rows, stride=pairs), :] = total[:, pair * LANES : (pair + 1) * LANES]
    out_ref[...] = wide_ref[...].astype(BF16)


def analysis(table, pieces, weight):
    parts, coefs, _ = table.shape
    shape = (coefs * weight.shape[1] // LANES, LANES)
    return vmem_call(
        functools.partial(analysis_kernel, parts),
        [table, *pieces, weight],
        jax.ShapeDtypeStruct(shape, BF16),
        [pltpu.VMEM(shape, F32)],
    )


def legendre_kernel(pairs, leg_ref, mask_ref, spec_ref, out_ref, wide_ref, lat_ref, back_ref):
    slots, nlat, _ = leg_ref.shape
    rows = 2 * pairs
    blocks = nlat // rows
    piece = 2 * slots * pairs
    low = low_lanes(blocks)
    wide_ref[...] = spec_ref[...].astype(F32)
    for slot in range(slots):
        lat = lat_ref.at[slot]

        def taken(part, pair):
            return pl.ds((part * slots + slot) * pairs + pair, blocks, stride=piece)

        for pair in range(pairs):
            even, odd = exchange(low, wide_ref[taken(0, pair), :], wide_ref[taken(1, pair), :])
            lat[pl.ds(2 * pair, blocks, stride=rows), :] = even
            lat[pl.ds(2 * pair + 1, blocks, stride=rows), :] = odd
        leg = leg_ref[slot]
        coeffs = lax.dot_general(
            lat[...].astype(BF16), leg, (((0,), (0,)), ((), ())), preferred_element_type=F32
        )
        coeffs = (coeffs * mask_ref[slot]).astype(BF16)
        lat[...] = lax.dot_general(leg, coeffs, (((1,), (1,)), ((), ())), preferred_element_type=F32)
        for pair in range(pairs):
            real, imag = exchange(
                low,
                lat[pl.ds(2 * pair, blocks, stride=rows), :],
                lat[pl.ds(2 * pair + 1, blocks, stride=rows), :],
            )
            back_ref[taken(0, pair), :] = real
            back_ref[taken(1, pair), :] = imag
    out_ref[...] = back_ref[...].astype(BF16)


def legendre_round_trip(legendre, mask, spectrum, pairs):
    slots, nlat, _ = legendre.shape
    return vmem_call(
        functools.partial(legendre_kernel, pairs),
        [legendre, mask, spectrum],
        jax.ShapeDtypeStruct(spectrum.shape, BF16),
        [
            pltpu.VMEM(spectrum.shape, F32),
            pltpu.VMEM((slots, nlat, LANES), F32),
            pltpu.VMEM(spectrum.shape, F32),
        ],
    )


def synthesis(table_ref, wide_ref, pairs):
    coefs = table_ref.shape[2]
    held = [wide_ref[pl.ds(pair, coefs, stride=pairs), :] for pair in range(pairs)]
    spectrum = jnp.concatenate(held, axis=1).astype(BF16)
    return [
        jnp.dot(table_ref[part], spectrum, preferred_element_type=F32)
        for part in range(table_ref.shape[0])
    ]


def synthesis_kernel(table_ref, *refs):
    wide_ref = refs[-1]
    count = len(refs) // 2
    for in_ref, out_ref in zip(refs[:count], refs[count:-1]):
        wide_ref[...] = in_ref[...].astype(F32)
        pairs = out_ref.shape[1]
        for part, grid in enumerate(synthesis(table_ref, wide_ref, pairs)):
            for pair in range(pairs):
                out_ref[part, pair] = grid[:, pair * LANES : (pair + 1) * LANES].astype(BF16)


def synthesize(table, *spectra):
    parts, cols, coefs = table.shape
    rows = spectra[0].shape[0]
    shape = jax.ShapeDtypeStruct((parts, rows // coefs, cols, LANES), BF16)
    return vmem_call(
        synthesis_kernel,
        [table, *spectra],
        [shape] * len(spectra),
        [pltpu.VMEM((rows, LANES), F32)],
    )


def finish_kernel(
    own_ref,
    west_ref,
    east_ref,
    far_west_ref,
    far_east_ref,
    table_ref,
    resp_ref,
    disco_ref,
    field_ref,
    cot_ref,
    weight_ref,
    out_ref,
    kept_ref,
    given_ref,
    wide_ref,
    mix_ref,
    slope_ref,
    total_ref,
):
    pairs, _, channels = field_ref.shape
    cols = table_ref.shape[1]
    middle = far_west_ref.shape[0]
    low = low_lanes(cols)
    place = lax.axis_index("lon")
    odd = lax.rem(place, 2) == 1
    near = place // 2
    wide_ref[:middle] = far_west_ref[...].astype(F32)
    wide_ref[middle:] = far_east_ref[...].astype(F32)
    far_grid = synthesis(table_ref, wide_ref, pairs)
    for pair in range(pairs):
        rows = slice(pair * 2 * cols, (pair + 1) * 2 * cols)
        mix = mix_ref.at[rows]
        for part in range(2):
            own, west, east = (
                ref[part, pair].astype(F32) for ref in (own_ref, west_ref, east_ref)
            )
            far = far_grid[part][:, pair * LANES : (pair + 1) * LANES]
            tiles = [
                (near, jnp.where(odd, west, own), jnp.where(odd, own, east)),
                (1 - near, jnp.where(odd, east, far), jnp.where(odd, far, west)),
            ]
            for tile, first, second in tiles:
                start = pl.multiple_of(part * channels + tile * LANES, LANES)
                grid = jnp.concatenate(exchange(low, first, second), axis=0).astype(BF16)
                mix[:, pl.ds(start, LANES)] = grid
        pre = jnp.dot(mix[...], weight_ref[...], preferred_element_type=F32) + disco_ref[pair]
        square = pre * pre
        bend = jnp.tanh(GELU_SCALE * (pre + GELU_CUBE * (square * pre)))
        activated = 0.5 * pre * (1.0 + bend)
        slope = 0.5 * (1.0 + bend) + 0.5 * pre * (1.0 - bend * bend) * (
            GELU_SCALE * (1.0 + 3.0 * GELU_CUBE * square)
        )
        out_ref[pair] = (field_ref[pair].astype(F32) + activated).astype(BF16)
        slope_ref[rows, :] = (cot_ref[pair].astype(F32) * slope).astype(BF16)
    start = 0
    for values_ref in [mix_ref] + [resp_ref.at[tap] for tap in range(resp_ref.shape[0])]:
        span = slice(start, start + values_ref.shape[1])
        start = span.stop
        total_ref[:, span] = lax.dot_general(
            slope_ref[...], values_ref[...], (((0,), (0,)), ((), ())), preferred_element_type=F32
        )
    first = lax.rem(lax.axis_index("lat"), 2) == 0
    half = kept_ref.shape[0]
    for start in range(0, half, LANES):
        span = slice(start, start + LANES)
        early = total_ref[:, span].T
        late = total_ref[:, half + start : half + start + LANES].T
        kept_ref[span, :] = jnp.where(first, early, late).astype(BF16)
        given_ref[span, :] = jnp.where(first, late, early).astype(BF16)


def finish(spectra, table, responses, disco_sum, field, cotangent, weight):
    rows, cols, channels = field.shape
    pairs = rows // 2
    grouped = (pairs, 2 * cols, channels)
    taps = responses.shape[0]
    stacked = weight.shape[0] + taps * channels
    half = jax.ShapeDtypeStruct((stacked // 2, channels), BF16)
    output, kept, given = vmem_call(
        finish_kernel,
        [
            *spectra,
            table,
            responses.reshape(taps, -1, channels),
            disco_sum.reshape(grouped),
            field.reshape(grouped),
            cotangent.reshape(grouped),
            weight,
        ],
        [jax.ShapeDtypeStruct(grouped, BF16), half, half],
        [
            pltpu.VMEM((pairs * table.shape[2], LANES), F32),
            pltpu.VMEM((rows * cols, weight.shape[0]), BF16),
            pltpu.VMEM((rows * cols, channels), BF16),
            pltpu.VMEM((channels, stacked), F32),
        ],
    )
    return output.reshape(field.shape), kept, given


def turn(value, axis, by):
    size = lax.axis_size(axis)
    return lax.ppermute(value, axis, [(i, (i + by) % size) for i in range(size)])


def disco_responses(above, field, below, support_blocks, filter_values):
    rows, cols, _ = field.shape
    lat_pos = lax.axis_index("lat")
    blocks = jnp.concatenate([above, field, below], axis=0)
    picks = support_blocks[0] - lat_pos + 1
    onehot = (picks[:, None] == jnp.arange(3, dtype=jnp.int32)[None, :]).astype(F32)
    operator = (
        jnp.einsum("tasb,sq->taqb", filter_values.astype(F32), onehot)
        .reshape(3, rows, 3 * rows)
        .astype(BF16)
    )
    here, level, there = (
        jnp.einsum("ab,boc->aoc", operator[tap], blocks, preferred_element_type=F32).astype(BF16)
        for tap in range(3)
    )
    first = turn(here[:, cols - 1 :], "lon", 1)
    last = turn(there[:, :1], "lon", -1)
    return jnp.stack(
        [
            jnp.concatenate([first, here[:, : cols - 1]], axis=1),
            level,
            jnp.concatenate([there[:, 1:], last], axis=1),
        ]
    )


def shares(value, axis, groups):
    return lax.all_to_all(value, axis, 0, 0, tiled=True, axis_index_groups=groups)


def sum_everywhere(kept, given):
    half, channels = kept.shape
    lon, lat = lax.axis_size("lon"), lax.axis_size("lat")
    side = 8 if lat % 8 == 0 else lat
    planes = [
        [(z * side + i) * lon + x for i in range(core, side, 2) for x in range(lon)]
        for z in range(lat // side)
        for core in range(2)
    ]
    columns = [list(range(i, lat, side)) for i in range(side)]
    count, depth = len(planes[0]), len(columns[0])

    def swap_cores(value):
        return lax.ppermute(value, "lat", [(i, i ^ 1) for i in range(lat)])

    def total(pieces):
        return jnp.sum(pieces.astype(F32), axis=0).astype(BF16)

    def copies(value, number):
        return jnp.broadcast_to(value[None], (number, *value.shape))

    core = lax.rem(lax.axis_index("lat"), 2)
    both = (kept.astype(F32) + swap_cores(given).astype(F32)).astype(BF16)
    share = half // count
    own = total(shares(both.reshape(count, share, channels), ("lat", "lon"), planes))
    own = total(shares(copies(own, depth), "lat", columns))
    mine = shares(copies(own, count), ("lat", "lon"), planes).reshape(half, channels)
    other = swap_cores(mine)
    first = jnp.where(core == 0, mine, other)
    second = jnp.where(core == 0, other, mine)
    return jnp.concatenate([first, second])


def local(
    field,
    cotangent,
    legendre,
    quad_weight,
    order_slots,
    support_blocks,
    filter_values,
    spectral_weight,
    disco_weight,
):
    rows, cols, channels = field.shape
    lat, lon = lax.axis_size("lat"), lax.axis_size("lon")
    nlon = cols * lon
    slots, nlat, degrees = legendre.shape
    pairs = rows // 2
    lat_pos, lon_pos = lax.axis_index("lat"), lax.axis_index("lon")

    pieces = pack(field)
    slabs = [pieces[0]] + [turn(pieces[k], "lon", k) for k in range(1, lon)]

    row_orders = jnp.broadcast_to(order_slots.reshape(lat, 1, slots), (lat, 2, slots)).reshape(-1)
    row_parts = jnp.broadcast_to(
        jnp.arange(2, dtype=jnp.int32)[None, :, None], (lat, 2, slots)
    ).reshape(-1)
    above, below = (
        with_layout_constraint(turn(field, "lat", way), Layout((0, 1, 2))) for way in (1, -1)
    )
    analysis_table, synthesis_table = fourier_tables(row_orders, row_parts, lon, pieces[0])
    lane_weight = jnp.repeat(quad_weight * (1.0 / nlon), HALF)[None, :]
    spectrum = analysis(analysis_table, slabs, lane_weight)
    own_orders = lax.dynamic_slice_in_dim(order_slots, lat_pos * slots, slots)
    mask = (jnp.arange(degrees, dtype=jnp.int32)[None, :] >= own_orders[:, None]).astype(F32)
    spectrum, mask = lax.optimization_barrier((spectrum, mask))
    spectrum = lax.all_to_all(
        spectrum.reshape(lat, -1, LANES), "lat", split_axis=0, concat_axis=0, tiled=True
    ).reshape(spectrum.shape)
    responses = disco_responses(above, field, below, support_blocks, filter_values)
    disco_sum = sum(
        jnp.dot(responses[tap].reshape(-1, channels), disco_weight[tap], preferred_element_type=F32)
        for tap in range(responses.shape[0])
    )
    spectrum, responses, disco_sum = lax.optimization_barrier((spectrum, responses, disco_sum))
    filtered = legendre_round_trip(legendre, mask[:, None, :], spectrum, pairs)
    filtered = lax.all_to_all(
        filtered.reshape(lat, -1, LANES), "lat", split_axis=0, concat_axis=0, tiled=True
    ).reshape(filtered.shape)
    west, east = turn(filtered, "lon", 1), turn(filtered, "lon", -1)
    middle = filtered.shape[0] // 2
    far_west, far_east = turn(west[:middle], "lon", 1), turn(east[middle:], "lon", -1)
    (own_grid,) = synthesize(synthesis_table, filtered)
    west_grid, east_grid = synthesize(synthesis_table, west, east)
    output, kept, given = finish(
        (own_grid, west_grid, east_grid, far_west, far_east),
        synthesis_table,
        responses,
        disco_sum,
        field,
        cotangent,
        spectral_weight.reshape(-1, channels),
    )
    sums = sum_everywhere(kept, given)
    spectral = spectral_weight.shape[0] * channels
    return (
        output,
        sums[:spectral].reshape(spectral_weight.shape).astype(F32),
        sums[spectral:].reshape(disco_weight.shape).astype(F32),
    )


def solution(mesh):
    placed = (
        P("lat", "lon", None),
        P("lat", "lon", None),
        P("lat", None, None),
        P("lat"),
        P(),
        P("lat", None),
        P(None, "lat", None, None),
        P(),
        P(),
    )
    return jax.shard_map(
        local,
        mesh=mesh,
        in_specs=placed,
        out_specs=(P("lat", "lon", None), P(), P()),
        check_vma=False,
    )
```
